32 devices in a mesh: dp: 8 (over y, x, core), tensor: 4 (over z).
Axes of the slice: x: 2, y: 2, z: 4, core: 2. Of those that a mesh axis runs over, the one named last changes fastest.
Arguments:
- hidden_in: bfloat16 [24576, 1536], P('dp', 'tensor'), may hold values from -6 to 6, as said below
- out_grad: bfloat16 [24576, 1536], P('dp', 'tensor'), may hold values from -6 to 6, as said below
- seq_lengths: int32 [16], replicated, may hold values from 256 to 3072, as said below
- seq_device: int32 [16], replicated, may hold values from 0 to 7, as said below
- seq_offset: int32 [16], replicated, may hold values from 0 to 2048, as said below
- norm_gain: float32 [1536], replicated, may hold values from 0.5 to 1.5
- w_gate: bfloat16 [1536, 3072], P(None, 'tensor'), may hold values from -0.15625 to 0.15625
- w_input: bfloat16 [1536, 3072], P(None, 'tensor'), may hold values from -0.15625 to 0.15625
- w_shared: bfloat16 [1536, 256], replicated, may hold values from -0.15625 to 0.15625
- w_step: bfloat16 [1536, 48], P(None, 'tensor'), may hold values from -0.15625 to 0.15625
- conv_inner: float32 [4, 3072], P(None, 'tensor'), may hold values from -3 to 3
- conv_shared: float32 [4, 256], replicated, may hold values from -3 to 3
- conv_inner_bias: float32 [3072], P('tensor'), may hold values from -0.5 to 0.5
- conv_shared_bias: float32 [256], replicated, may hold values from -0.5 to 0.5
- step_bias: float32 [48], P('tensor'), may hold values from -6 to -2
- decay_log: float32 [48], P('tensor'), may hold values from -7 to 1
- skip_gain: float32 [48], P('tensor'), may hold values from 0.5 to 2
- gate_norm_gain: float32 [3072], P('tensor'), may hold values from 0.5 to 1.5
- w_output: bfloat16 [3072, 1536], P('tensor'), may hold values from -0.109375 to 0.109375
Outputs:
- mixed_out: bfloat16 [24576, 1536], P('dp', 'tensor')
- hidden_grad: float32 [24576, 1536], P('dp', 'tensor')
- norm_gain_grad: float32 [1536], replicated
- w_gate_grad: float32 [1536, 3072], P(None, 'tensor')
- w_input_grad: float32 [1536, 3072], P(None, 'tensor')
- w_shared_grad: float32 [1536, 256], replicated
- w_step_grad: float32 [1536, 48], P(None, 'tensor')
- conv_inner_grad: float32 [4, 3072], P(None, 'tensor')
- conv_shared_grad: float32 [4, 256], replicated
- conv_inner_bias_grad: float32 [3072], P('tensor')
- conv_shared_bias_grad: float32 [256], replicated
- step_bias_grad: float32 [48], P('tensor')
- decay_log_grad: float32 [48], P('tensor')
- skip_gain_grad: float32 [48], P('tensor')
- gate_norm_gain_grad: float32 [3072], P('tensor')
- w_output_grad: float32 [3072, 1536], P('tensor')
The draws below stay inside these ranges and needn't reach their ends.
Inputs may be any that keep to these rules, and one draw needn't show every extreme that they name: `hidden_in`: entries are independent, of deviation one. `out_grad`: entries are independent, of deviation one. `seq_lengths`: lengths are multiples of 256; some sequence has exactly 3072 rows. `seq_device`: half of the dp indices hold one sequence and half hold three; every index holds one or more. Sequence numbers follow no order. `seq_offset`: offsets are multiples of 256; the sequences of one dp index lie end to end from its row 0, and offset plus length is at most 3072; the largest offset is reached.
All inputs are finite; a program needn't handle non-finite values.
Results may differ from the reference program's by a relative error of at most 0.012.
The reference program's roundings to bfloat16 on the way count: a program that leaves them out, or rounds other values in their place, can miss the bound.
Values may be sent and summed in bfloat16 or wider, within the bound.
No kernel may reach another device: no remote copies, remote signals or barrier semaphores. Data moves between devices by JAX's collectives and lax.ppermute only.
A program may use at most 320 MiB of HBM per device.

```python
import jax
import jax.numpy as jnp
from jax import lax

D = 1536
HEADS = 48
DSTATE = 128
CONV_TAPS = 4
BLOCK_LEN = 256
BLOCKS_DEV = 12
DINNER = 3072
ROWS_DEV = 3072
TOKENS = 24576
NSEQ = 16
N_DP = 8


def seq_layout(key):
    device_count = NSEQ // 2
    key_order, key_length, key_ids = jax.random.split(key, 3)
    ranking = jax.random.permutation(key_order, device_count)
    single = ranking < device_count // 2
    counts = jnp.where(single, 1, 3)
    highest = jnp.where(single, BLOCKS_DEV, BLOCKS_DEV // 3)
    raw_draw = jax.random.randint(key_length, (device_count, 3), 0, 1 << 20)
    blocks = 1 + raw_draw % highest[:, None]
    slot_ids = jnp.arange(3)[None, :]
    blocks = jnp.where((ranking == 0)[:, None] & (slot_ids == 0), BLOCKS_DEV, blocks)
    blocks = jnp.where((ranking == device_count // 2)[:, None] & (slot_ids < 2), BLOCKS_DEV // 3, blocks)
    filled = slot_ids < counts[:, None]
    blocks = jnp.where(filled, blocks, 0)
    starts = jnp.cumsum(blocks, axis=1) - blocks
    flat_live = filled.reshape(-1)
    slot_rank = jnp.cumsum(flat_live.astype(jnp.int32)) - 1
    shuffled = jax.random.permutation(key_ids, NSEQ)
    target = jnp.where(flat_live, shuffled[jnp.where(flat_live, slot_rank, 0)], NSEQ)
    owners = jnp.broadcast_to(jnp.arange(device_count)[:, None], (device_count, 3)).reshape(-1)
    empty = jnp.zeros((NSEQ + 1,), jnp.int32)
    lengths = empty.at[target].set((blocks * BLOCK_LEN).reshape(-1).astype(jnp.int32))[:NSEQ]
    devices = empty.at[target].set(owners.astype(jnp.int32))[:NSEQ]
    offsets = empty.at[target].set((starts * BLOCK_LEN).reshape(-1).astype(jnp.int32))[:NSEQ]
    return (lengths, devices, offsets)


def draw_seq_lengths(key, part):
    return seq_layout(key)[0]


def draw_seq_device(key, part):
    return seq_layout(key)[1]


def draw_seq_offset(key, part):
    return seq_layout(key)[2]


def draw_hidden_in(key, part):
    key = jax.random.fold_in(key, 11)
    return jnp.clip(jax.random.normal(key, (TOKENS, D), jnp.float32), -6.0, 6.0).astype(jnp.bfloat16)


def draw_out_grad(key, part):
    key = jax.random.fold_in(key, 23)
    return jnp.clip(jax.random.normal(key, (TOKENS, D), jnp.float32), -6.0, 6.0).astype(jnp.bfloat16)


def levels(own_key, extent, shards, least, high):
    level = 1.0
    for position, shards_of in shards:
        heights = jax.random.uniform(jax.random.fold_in(jax.random.fold_in(own_key, 6), position), (shards_of,), jnp.float32, least / len(shards), high / len(shards))
        level = level * jnp.repeat(jnp.exp(heights), extent[position] // shards_of).reshape((-1,) + (1,) * (len(extent) - 1 - position))
    return level


def normal_values(own_key, extent, scale, most, shards=(), kind=jnp.bfloat16):
    gain = levels(own_key, extent, shards, -0.22, 0.18) if shards else 1.0
    entries = jax.random.normal(own_key, extent, jnp.float32) * scale * gain
    return jnp.minimum(jnp.maximum(entries, -most), most).astype(kind)


def setup_inputs(seed: int = 0) -> dict:
    keys = jax.random.split(jax.random.key(seed), 20)
    return {
        "hidden_in": draw_hidden_in(jax.random.fold_in(keys[19], 71), 0),
        "out_grad": draw_out_grad(jax.random.fold_in(keys[19], 71), 0),
        "seq_lengths": draw_seq_lengths(jax.random.fold_in(keys[19], 71), 0),
        "seq_device": draw_seq_device(jax.random.fold_in(keys[19], 71), 0),
        "seq_offset": draw_seq_offset(jax.random.fold_in(keys[19], 71), 0),
        "norm_gain": jnp.clip(1.0 + 0.1 * jax.random.normal(keys[5], (D,), jnp.float32), 0.5, 1.5),
        "w_gate": normal_values(keys[6], (D, DINNER), D ** -0.5, 0.15625, ((1, 4),)),
        "w_input": normal_values(keys[7], (D, DINNER), D ** -0.5, 0.15625, ((1, 4),)),
        "w_shared": normal_values(keys[8], (D, 2 * DSTATE), D ** -0.5, 0.15625),
        "w_step": normal_values(keys[9], (D, HEADS), D ** -0.5, 0.15625, ((1, 4),)),
        "conv_inner": normal_values(keys[10], (CONV_TAPS, DINNER), CONV_TAPS ** -0.5, 3.0, ((1, 4),), jnp.float32),
        "conv_shared": normal_values(keys[11], (CONV_TAPS, 2 * DSTATE), CONV_TAPS ** -0.5, 3.0, (), jnp.float32),
        "conv_inner_bias": jnp.clip(jax.random.uniform(keys[12], (DINNER,), jnp.float32, -0.5, 0.5) * levels(keys[12], (DINNER,), ((0, 4),), -0.4, 0.0), -0.5, 0.5),
        "conv_shared_bias": jnp.clip(jax.random.uniform(keys[13], (2 * DSTATE,), jnp.float32, -0.5, 0.5), -0.5, 0.5),
        "step_bias": jnp.clip(-6.0 + 4.0 * jax.random.uniform(keys[14], (HEADS,), jnp.float32) ** levels(keys[14], (HEADS,), ((0, 4),), -0.2, 0.2), -6.0, -2.0),
        "decay_log": jnp.clip(-7.0 + 8.0 * jax.random.uniform(keys[15], (HEADS,), jnp.float32) ** levels(keys[15], (HEADS,), ((0, 4),), -0.2, 0.2), -7.0, 1.0),
        "skip_gain": jnp.clip(0.5 + 1.5 * jax.random.uniform(keys[16], (HEADS,), jnp.float32) ** levels(keys[16], (HEADS,), ((0, 4),), -0.2, 0.2), 0.5, 2.0),
        "gate_norm_gain": jnp.clip(1.0 + 0.1 * jax.random.normal(keys[17], (DINNER,), jnp.float32), 0.5, 1.5),
        "w_output": normal_values(keys[18], (DINNER, D), DINNER ** -0.5, 0.109375, ((0, 4),)),
    }


@jax.custom_vjp
def low(v):
    return lax.optimization_barrier(v.astype(jnp.bfloat16)).astype(jnp.float32)

@jax.custom_vjp
def low_back(v):
    return v

def low_keep(v):
    return (low(v), None)

def low_pass(kept, grad):
    return (grad,)

def back_keep(v):
    return (v, None)

def back_low(kept, grad):
    return (low(grad),)
low.defvjp(low_keep, low_pass)
low_back.defvjp(back_keep, back_low)
PRECISE = lax.Precision.HIGHEST
epsilon = 1e-05

def matmul(left_side, right_side):
    return jnp.dot(left_side, right_side, precision=PRECISE, preferred_element_type=jnp.float32)

def swish_act(values):
    return values * jax.nn.sigmoid(values)

def row_layout(lengths, owners, offsets, device_index, row_count):
    row_ids = jnp.arange(row_count, dtype=jnp.int32)[:, None]
    inside = (owners[None, :] == device_index) & (row_ids >= offsets[None, :]) & (row_ids < offsets[None, :] + lengths[None, :])
    positions = lax.optimization_barrier(jnp.sum(jnp.where(inside, row_ids - offsets[None, :], 0), axis=1)).astype(jnp.int32)
    live_rows = lax.optimization_barrier(jnp.sum(inside.astype(jnp.float32), axis=1))
    return (positions, live_rows)

def causal_conv(values, kernel, offset_bias, positions):
    row_count = values.shape[0]
    taps = kernel.shape[0]
    summed = offset_bias[None, :] + kernel[taps - 1][None, :] * values
    for lag_steps in range(1, taps):
        shifted = jnp.pad(values, ((lag_steps, 0), (0, 0)))[:row_count]
        allowed = (positions >= lag_steps).astype(jnp.float32)[:, None]
        summed = summed + kernel[taps - 1 - lag_steps][None, :] * shifted * allowed
    return swish_act(summed)

def state_space(inner_vals, step_sizes, decays, input_map, output_map, fresh_block):
    row_count, head_count, head_width = inner_vals.shape
    block_count = row_count // BLOCK_LEN
    values = inner_vals.reshape(block_count, BLOCK_LEN, head_count, head_width)
    deltas = step_sizes.reshape(block_count, BLOCK_LEN, head_count)
    cumulative = jnp.cumsum(decays.reshape(block_count, BLOCK_LEN, head_count), axis=1)
    inputs_b = input_map.reshape(block_count, BLOCK_LEN, -1)
    outputs_c = output_map.reshape(block_count, BLOCK_LEN, -1)
    causal = (jnp.arange(BLOCK_LEN)[:, None] >= jnp.arange(BLOCK_LEN)[None, :])[None, None]
    by_head = jnp.swapaxes(cumulative, 1, 2)
    spread = by_head[:, :, :, None] - by_head[:, :, None, :]
    decay_map = jnp.where(causal, jnp.exp(jnp.where(causal, spread, 0.0)), 0.0)
    intersection = jnp.einsum('ctn,csn->cts', outputs_c, inputs_b, precision=PRECISE)
    mixing = decay_map * intersection[:, None] * jnp.swapaxes(deltas, 1, 2)[:, :, None, :]
    within = jnp.einsum('chts,cshp->cthp', mixing, values, precision=PRECISE)
    to_end = jnp.exp(cumulative[:, -1:, :] - cumulative) * deltas
    block_states = jnp.einsum('csn,csh,cshp->chnp', inputs_b, to_end, values, precision=PRECISE)
    block_decay = jnp.exp(cumulative[:, -1, :])

    def carry_step(carried, carry_item):
        is_fresh, decay_total, state_add = carry_item
        entering = jnp.where(is_fresh, jnp.zeros_like(carried), carried)
        return (decay_total[:, None, None] * entering + state_add, entering)
    initial = jnp.zeros(block_states.shape[1:], jnp.float32)
    final_state, entering_all = lax.scan(carry_step, initial, (fresh_block, block_decay, block_states))
    across = jnp.einsum('ctn,cth,chnp->cthp', outputs_c, jnp.exp(cumulative), entering_all, precision=PRECISE)
    return (within + across).reshape(row_count, head_count, head_width)

def mixer_core(inner_proj, shared_proj, raw_step, conv_inner, conv_shared, conv_inner_bias, conv_shared_bias, step_bias, decay_log, skip_gain, positions):
    head_count = raw_step.shape[1]
    row_count = inner_proj.shape[0]
    inner_conv = causal_conv(inner_proj, conv_inner, conv_inner_bias, positions)
    shared_conv = causal_conv(shared_proj, conv_shared, conv_shared_bias, positions)
    state_width = shared_conv.shape[1] // 2
    step_sizes = jax.nn.softplus(raw_step + step_bias[None, :])
    decays = -step_sizes * jnp.exp(decay_log)[None, :]
    fresh_block = positions[::BLOCK_LEN] == 0
    by_heads = inner_conv.reshape(row_count, head_count, -1)
    scanned = state_space(by_heads, step_sizes, decays, shared_conv[:, :state_width], shared_conv[:, state_width:], fresh_block)
    return (scanned + skip_gain[None, :, None] * by_heads).reshape(row_count, -1)

def block_forward(source, weights, positions, live_rows):
    norm_gain, w_gate, w_input, w_shared, w_step, conv_inner, conv_shared, conv_inner_bias, conv_shared_bias, step_bias, decay_log, skip_gain, gate_norm_gain, w_output = weights
    factor = lax.rsqrt(lax.optimization_barrier(jnp.mean(source * source, axis=1, keepdims=True)) + epsilon)
    normed = low(source * factor * norm_gain[None, :])
    gate_proj = low_back(matmul(normed, w_gate))
    inner_proj = low_back(matmul(normed, w_input))
    shared_proj = low_back(matmul(normed, w_shared))
    raw_step = low_back(matmul(normed, w_step))
    scan_out = mixer_core(inner_proj, shared_proj, raw_step, conv_inner, conv_shared, conv_inner_bias, conv_shared_bias, step_bias, decay_log, skip_gain, positions)
    gated = scan_out * swish_act(gate_proj)
    gate_scale = lax.rsqrt(lax.optimization_barrier(jnp.mean(gated * gated, axis=1, keepdims=True)) + epsilon)
    normed_y = low(gated * gate_scale * gate_norm_gain[None, :])
    return source + live_rows[:, None] * matmul(normed_y, w_output)

def reference(hidden_in, out_grad, seq_lengths, seq_device, seq_offset, norm_gain, w_gate, w_input, w_shared, w_step, conv_inner, conv_shared, conv_inner_bias, conv_shared_bias, step_bias, decay_log, skip_gain, gate_norm_gain, w_output):
    params = tuple((weight.astype(jnp.float32) for weight in (norm_gain, w_gate, w_input, w_shared, w_step, conv_inner, conv_shared, conv_inner_bias, conv_shared_bias, step_bias, decay_log, skip_gain, gate_norm_gain, w_output)))
    blocks_in = hidden_in.astype(jnp.float32).reshape(N_DP, ROWS_DEV, D)
    blocks_grad = out_grad.astype(jnp.float32).reshape(N_DP, ROWS_DEV, D)

    def one_block(accum, block_item):
        device_index, block_in, block_grad = block_item
        positions, live_rows = row_layout(seq_lengths, seq_device, seq_offset, device_index, ROWS_DEV)

        def forward_fn(block_values, *weights):
            return block_forward(block_values, weights, positions, live_rows)
        result, pullback = jax.vjp(forward_fn, block_in, *params)
        grads = pullback(block_grad)
        accum = jax.tree.map(jnp.add, accum, tuple(grads[1:]))
        return (accum, (result.astype(jnp.bfloat16), grads[0]))
    initial = tuple((jnp.zeros_like(weight) for weight in params))
    sums, (results, input_grads) = lax.scan(one_block, initial, (jnp.arange(N_DP, dtype=jnp.int32), blocks_in, blocks_grad))
    return (results.reshape(TOKENS, D), input_grads.reshape(TOKENS, D), sums[0], sums[1], sums[2], sums[3], sums[4], sums[5], sums[6], sums[7], sums[8], sums[9], sums[10], sums[11], sums[12], sums[13])
```

```python
import functools

import jax
import jax.numpy as jnp
from jax import lax
from jax.experimental import pallas as pl
from jax.experimental.pallas import tpu as pltpu
from jax.sharding import PartitionSpec as P

F32 = jnp.float32
BF16 = jnp.bfloat16
PRECISE = lax.Precision.HIGHEST
EPSILON = 1e-05
LEN = 128
HALO = 16
WIDE = 256
VMEM = 52 * 1024 * 1024


def dot_nn(a, b):
    return jnp.dot(a, b, preferred_element_type=F32)


def dot_nt(a, b):
    return lax.dot_general(a, b, (((1,), (1,)), ((), ())), preferred_element_type=F32)


def dot_tn(a, b):
    return lax.dot_general(a, b, (((0,), (0,)), ((), ())), preferred_element_type=F32)


def sigmoid(v):
    return 1.0 / (1.0 + jnp.exp(-v))


def split_pair(v):
    lane = lax.broadcasted_iota(jnp.int32, v.shape, 1)
    high = v.astype(BF16).astype(F32)
    return jnp.where(lane < 64, high, v - high).astype(BF16)


def split_triple(v):
    lane = lax.broadcasted_iota(jnp.int32, v.shape, 1)
    high = v.astype(BF16).astype(F32)
    rest = v - high
    middle = rest.astype(BF16).astype(F32)
    return jnp.where(lane < 64, high, jnp.where(lane < 128, middle, rest - middle)).astype(BF16)


def head_sums(v, select):
    high = v.astype(BF16)
    low = (v - high.astype(F32)).astype(BF16)
    return dot_nn(high, select) + dot_nn(low, select)


def halves(v):
    high = v.astype(BF16)
    return high, (v - high.astype(F32)).astype(BF16)


def finer(dot, a, b):
    a_high, a_low = halves(a)
    b_high, b_low = halves(b)
    return dot(a_high, b_high) + (dot(a_high, b_low) + dot(a_low, b_high))


def fold(v):
    total = v[:, :128]
    for i in range(1, v.shape[1] // 128):
        total = total + v[:, i * 128 : (i + 1) * 128]
    return total


def chunk(i, width):
    return pl.ds(pl.multiple_of(i * width, width), width)


def conv_states_kernel(
    keep_ref, ip_ref, halo_ref, taps_ref, bias_ref, b_ref, coef_ref, dec_ref, spread_ref,
    u_ref, local_ref, out_ref, ext_ref, state_ref,
):
    c = pl.program_id(0)
    keep = keep_ref[c].astype(F32)

    @pl.when(c == 0)
    def _():
        state_ref[...] = jnp.zeros_like(state_ref)
        ext_ref[0:8, :] = halo_ref[8:16, :] * keep

    @pl.when(c > 0)
    def _():
        ext_ref[0:8, :] = ext_ref[LEN : LEN + 8, :] * keep

    ext_ref[8 : LEN + 8, :] = ip_ref[...]
    coef = split_pair(coef_ref[...])
    b_map, b_low = halves(b_ref[...])

    def step(i, carry):
        at = chunk(i, WIDE)
        u = bias_ref[:, at] + taps_ref[3:4, at] * ext_ref[8 : 8 + LEN, at]
        for lag in range(1, 4):
            u = u + taps_ref[3 - lag : 4 - lag, at] * ext_ref[8 - lag : 8 - lag + LEN, at]
        u_ref[:, at] = u
        w = u * sigmoid(u) * dot_nn(coef, spread_ref[:, at])
        state = state_ref[:, at] * keep
        local_ref[0, :, at] = state.astype(BF16)
        state_ref[:, at] = dec_ref[0, :, at] * state + (dot_tn(b_map, w.astype(BF16))+dot_tn(b_low, w.astype(BF16)))
        return carry

    lax.fori_loop(0, u_ref.shape[1] // WIDE, step, 0)

    @pl.when(c == pl.num_programs(0) - 1)
    def _():
        out_ref[...] = state_ref[...]


def within_kernel(
    u_ref, cum_ref, cum_t_ref, step_ref, b_ref, c_ref, columns_ref, spread_ref, y_ref
):
    scores = finer(dot_nt, c_ref[...], b_ref[...])
    row = lax.broadcasted_iota(jnp.int32, (LEN, LEN), 0)
    col = lax.broadcasted_iota(jnp.int32, (LEN, LEN), 1)
    scores = jnp.where(row >= col, scores, 0.0)
    scores = jnp.concatenate([scores, scores], axis=1)
    cum = split_triple(cum_ref[...])
    steps = split_pair(step_ref[...])
    first = col < 64

    def pair(p, carry):
        at = chunk(p, 128)
        left = dot_nn(cum, columns_ref[:, chunk(p, 256)])
        right = jnp.concatenate(
            [cum_t_ref[pl.ds(2 * p, 1), :], cum_t_ref[pl.ds(2 * p + 1, 1), :]], axis=1
        )
        mixing = (jnp.exp(jnp.minimum(left - right, 0.0)) * scores).astype(BF16)
        u = u_ref[:, at]
        v = u * sigmoid(u) * dot_nn(steps, spread_ref[:, at])
        stacked = jnp.concatenate(
            [jnp.where(first, v, 0.0).astype(BF16), jnp.where(first, 0.0, v).astype(BF16)], axis=0
        )
        y_ref[:, at] = dot_nn(mixing, stacked)
        return carry

    lax.fori_loop(0, u_ref.shape[1] // 128, pair, 0, unroll=2)


def gate_kernel(
    keep_ref, y_ref, u_ref, gate_ref, ng_ref, local_ref, enter_ref, pref_ref, c_ref, grow_ref,
    skip_ref, gain_ref, dec_ref, spread_ref, select_ref,
    ny_ref, dy_ref, gg_ref, q_ref, dc_ref, gain_grad_ref, skip_grad_ref, out_ref,
    scan_ref, carried_ref, state_ref,
):
    g = pl.program_id(0)
    c = pl.num_programs(0) - 1 - g
    width = y_ref.shape[1]
    keep = keep_ref[c].astype(F32)

    @pl.when(g == 0)
    def _():
        state_ref[...] = jnp.zeros_like(state_ref)
        gain_grad_ref[...] = jnp.zeros_like(gain_grad_ref)
        skip_grad_ref[...] = jnp.zeros_like(skip_grad_ref)

    c_map, c_low = halves(c_ref[...])
    grow = split_pair(grow_ref[...])

    def forward(i, sums):
        squares, stat = sums
        at = chunk(i, WIDE)
        carried = (
            local_ref[0, :, at].astype(F32) + pref_ref[0, :, at] * enter_ref[:, at].astype(F32)
        ).astype(BF16)
        carried_ref[:, at] = carried
        scanned = y_ref[:, at] + dot_nn(grow, spread_ref[:, at]) * (dot_nn(c_map, carried)+dot_nn(c_low,carried))
        scan_ref[:, at] = scanned
        u = u_ref[:, at]
        y = scanned + skip_ref[:, at] * (u * sigmoid(u))
        gate = gate_ref[:, at]
        gated = y * (gate * sigmoid(gate))
        squares = squares + fold(gated * gated)
        stat = stat + fold(ng_ref[:, at] * gain_ref[:, at] * gated)
        return (squares, stat)

    nothing = jnp.zeros((LEN, 128), F32)
    squares, stat = lax.fori_loop(0, width // WIDE, forward, (nothing, nothing))
    scale = lax.rsqrt(jnp.sum(squares, axis=1, keepdims=True) / width + EPSILON)
    back = scale * scale * scale * (jnp.sum(stat, axis=1, keepdims=True) / width)

    def backward(i, sums):
        q, dc = sums
        at = chunk(i, WIDE)
        scanned = scan_ref[:, at]
        u = u_ref[:, at]
        x = u * sigmoid(u)
        y = scanned + skip_ref[:, at] * x
        gate = gate_ref[:, at]
        open_ = sigmoid(gate)
        act = gate * open_
        gated = y * act
        scaled = gated * scale
        ng = ng_ref[:, at]
        gain = gain_ref[:, at]
        ny_ref[:, at] = (scaled * gain).astype(BF16)
        gain_grad_ref[:, at] += jnp.sum(ng * scaled, axis=0, keepdims=True)
        gated_grad = scale * (ng * gain) - gated * back
        gg_ref[:, at] = (gated_grad * y * open_ * (1.0 + gate * (1.0 - open_))).astype(BF16)
        dy_low = (gated_grad * act).astype(BF16)
        dy_ref[:, at] = dy_low
        dy = dy_low.astype(F32)
        skip_grad_ref[:, at] += jnp.sum(dy * x, axis=0, keepdims=True)
        q = q + head_sums(dy * scanned, select_ref[chunk(i, WIDE), :])
        z = (dot_nn(grow, spread_ref[:, at]) * dy).astype(BF16)
        dc = dc + dot_nt(z, carried_ref[:, at])
        state_ref[:, at] = keep * (dec_ref[0, :, at] * state_ref[:, at] + (dot_tn(c_map, z)+dot_tn(c_low,z)))
        return (q, dc)

    q, dc = lax.fori_loop(0, width // WIDE, backward, (nothing, nothing))
    q_ref[...] = q
    dc_ref[...] = dc

    @pl.when(c == 0)
    def _():
        out_ref[...] = state_ref[...]


def within_back_kernel(
    u_ref, dy_ref, cum_ref, cum_t_ref, step_ref, b_ref, c_ref, columns_ref, spread_ref,
    dv_ref, db_ref, dc_ref,
):
    scores = finer(dot_nt, b_ref[...], c_ref[...])
    row = lax.broadcasted_iota(jnp.int32, (LEN, LEN), 0)
    col = lax.broadcasted_iota(jnp.int32, (LEN, LEN), 1)
    scores = jnp.where(row <= col, scores, 0.0)
    scores = jnp.concatenate([scores, scores], axis=1)
    cum = split_triple(cum_ref[...])
    steps = split_pair(step_ref[...])
    first = col < 64

    def pair(p, total):
        at = chunk(p, 128)
        left = dot_nn(cum, columns_ref[:, chunk(p, 256)])
        right = jnp.concatenate(
            [cum_t_ref[pl.ds(2 * p, 1), :], cum_t_ref[pl.ds(2 * p + 1, 1), :]], axis=1
        )
        decay = jnp.exp(jnp.minimum(right - left, 0.0))
        mixing = (decay * scores).astype(BF16)
        dy_low = dy_ref[:, at]
        dy = dy_low.astype(F32)
        dy_stack = jnp.concatenate(
            [jnp.where(first, dy, 0.0).astype(BF16), jnp.where(first, 0.0, dy).astype(BF16)], axis=0
        )
        dv_ref[:, at] = dot_nn(mixing, dy_stack)
        u = u_ref[:, at]
        v = u * sigmoid(u) * dot_nn(steps, spread_ref[:, at])
        v_stack = jnp.concatenate(
            [jnp.where(first, v, 0.0).astype(BF16), jnp.where(first, 0.0, v).astype(BF16)], axis=0
        )
        dw = dot_nt(v_stack, dy_low)
        return total + decay[:, :LEN] * dw[:LEN] + decay[:, LEN:] * dw[LEN:]

    total = lax.fori_loop(
        0, u_ref.shape[1] // 128, pair, jnp.zeros((LEN, LEN), F32), unroll=2
    )
    total = jnp.where(row <= col, total, 0.0)
    db_ref[...] = finer(dot_nn, total, c_ref[...])
    dc_ref[...] = finer(dot_tn, total, b_ref[...])


def across_back_kernel(
    keep_ref, u_ref, dy_ref, dv_ref, ip_ref, halo_ref, local_ref, enter_ref, pref_ref, leave_ref,
    b_ref, c_ref, grow_ref, fall_ref, step_ref, skip_ref, dec_ref, taps_ref, spread_ref, select_ref,
    ig_ref, db_ref, q_ref, r_ref, end_ref, taps_grad_ref, bias_grad_ref, head_ref,
    state_ref, ext_ref,
):
    g = pl.program_id(0)
    c = pl.num_programs(0) - 1 - g
    width = u_ref.shape[1]
    keep = keep_ref[c].astype(F32)

    @pl.when(g == 0)
    def _():
        state_ref[...] = leave_ref[...].astype(F32)
        taps_grad_ref[...] = jnp.zeros_like(taps_grad_ref)
        bias_grad_ref[...] = jnp.zeros_like(bias_grad_ref)
        ext_ref[LEN : LEN + 8, :] = jnp.zeros((8, width), F32)

    @pl.when(g > 0)
    def _():
        ext_ref[LEN : LEN + 8, :] = ext_ref[0:8, :] * keep_ref[c + 1].astype(F32)

    b_map, b_low = halves(b_ref[...])
    c_map, c_low = halves(c_ref[...])
    grow = split_pair(grow_ref[...])
    fall = split_pair(fall_ref[...])
    steps = split_pair(step_ref[...])

    def step(i, sums):
        db, q, r = sums
        at = chunk(i, WIDE)
        spread = spread_ref[:, at]
        state = state_ref[:, at]
        state_low = state.astype(BF16)
        falling = dot_nn(fall, spread)
        across = falling * (dot_nn(b_map, state_low)+dot_nn(b_low, state_low))
        dv = dv_ref[:, at] + across
        u = u_ref[:, at]
        open_ = sigmoid(u)
        x = u * open_
        delta = dot_nn(steps, spread)
        v = x * delta
        v_low = v.astype(BF16).astype(F32)
        dy = dy_ref[:, at].astype(F32)
        dx = delta * dv + skip_ref[:, at] * dy
        ext_ref[0:LEN, at] = dx * (open_ * (1.0 + u * (1.0 - open_)))
        select = select_ref[chunk(i, WIDE), :]
        q = q + head_sums(v_low * dv, select)
        r = r + head_sums(x * dv, select)
        carried = (
            local_ref[0, :, at].astype(F32) + pref_ref[0, :, at] * enter_ref[:, at].astype(F32)
        ).astype(BF16)
        decay = dec_ref[0, :, at]
        end_ref[0, :, at] = jnp.sum(v_low * across, axis=0, keepdims=True) + decay * jnp.sum(
            state * carried.astype(F32), axis=0, keepdims=True
        )
        db = db + dot_nt((falling * v).astype(BF16), state_low)
        z = (dot_nn(grow, spread) * dy).astype(BF16)
        state_ref[:, at] = keep * (decay * state + (dot_tn(c_map, z)+dot_tn(c_low,z)))
        return (db, q, r)

    nothing = jnp.zeros((LEN, 128), F32)
    db, q, r = lax.fori_loop(0, width // WIDE, step, (nothing, nothing, nothing))
    db_ref[...] = db
    q_ref[...] = q
    r_ref[...] = r

    def conv(i, carry):
        at = chunk(i, WIDE)
        ip = ip_ref[:, at]
        du = ext_ref[0:LEN, at]
        bias_grad_ref[:, at] += jnp.sum(du, axis=0, keepdims=True)
        total = taps_ref[3:4, at] * du
        taps_grad_ref[3:4, at] += jnp.sum(ip * du, axis=0, keepdims=True)
        for lag in range(1, 4):
            later = ext_ref[lag : lag + LEN, at]
            total = total + taps_ref[3 - lag : 4 - lag, at] * later
            taps_grad_ref[3 - lag : 4 - lag, at] += jnp.sum(ip * later, axis=0, keepdims=True)
        ig_ref[:, at] = total.astype(BF16)
        return carry

    lax.fori_loop(0, width // WIDE, conv, 0)

    @pl.when(c == 0)
    def _():
        head_ref[...] = ext_ref[0:8, :] * keep
        for lag in range(1, 4):
            part = keep * ext_ref[0:lag, :] * halo_ref[HALO - lag : HALO, :]
            taps_grad_ref[3 - lag : 4 - lag, :] += jnp.sum(part, axis=0, keepdims=True)


def place_kernel(copies, count, where_ref, *refs):
    pieces, out_ref = refs[:count], refs[count]
    stages, sems = refs[count + 1 : -1], refs[-1]
    loads = []
    for i, piece in enumerate(pieces):
        for t in range(piece.shape[0]):
            load = pltpu.make_async_copy(piece.at[t], stages[i].at[t], sems.at[0, i, t])
            load.start()
            loads.append((i, t, load))
    stores = []
    for i, t, load in loads:
        load.wait()
        rows, cols = pieces[i].shape[1:]
        row_slot, col_slot = copies[i][t]
        row = pl.multiple_of(where_ref[row_slot], 16)
        if col_slot is None:
            target = out_ref.at[pl.ds(row, rows)]
        else:
            col = pl.multiple_of(where_ref[col_slot], 128)
            target = out_ref.at[pl.ds(row, rows), pl.ds(col, cols)]
        store = pltpu.make_async_copy(stages[i].at[t], target, sems.at[1, i, t])
        store.start()
        stores.append(store)
    for store in stores:
        store.wait()


def place(pieces, rows_of, cols_of, shape):
    slots, copies = [], []
    whole = pieces[0].shape[2] == shape[1]
    for i, piece in enumerate(pieces):
        row = []
        for t in range(piece.shape[0]):
            slots.append(jnp.asarray(rows_of[i][t], jnp.int32))
            row_slot = len(slots) - 1
            col_slot = None
            if not whole:
                slots.append(jnp.asarray(cols_of[i][t], jnp.int32))
                col_slot = len(slots) - 1
            row.append((row_slot, col_slot))
        copies.append(row)
    anywhere = pl.BlockSpec(memory_space=pl.ANY)
    nbytes = 2 * shape[0] * shape[1] * 2
    return pl.pallas_call(
        functools.partial(place_kernel, copies, len(pieces)),
        in_specs=[pl.BlockSpec(memory_space=pltpu.SMEM)] + [anywhere] * len(pieces),
        out_specs=anywhere,
        out_shape=jax.ShapeDtypeStruct(shape, pieces[0].dtype),
        scratch_shapes=[pltpu.VMEM(piece.shape, piece.dtype) for piece in pieces]
        + [pltpu.SemaphoreType.DMA((2, len(pieces), pieces[0].shape[0]))],
        compiler_params=pltpu.CompilerParams(vmem_limit_bytes=VMEM),
        cost_estimate=pl.CostEstimate(flops=0, bytes_accessed=nbytes, transcendentals=0),
        name="place",
    )(jnp.stack(slots), *pieces)


def norm_kernel(rot_ref, gain_ref, *refs):
    pieces, (hid_ref, normed_ref) = refs[:-2], refs[-2:]
    width = pieces[0].shape[1]
    squares = jnp.zeros((pieces[0].shape[0], 128), F32)
    for piece in pieces:
        v = piece[...].astype(F32)
        squares = squares + fold(v * v)
    mean = jnp.sum(squares, axis=1, keepdims=True) / (width * len(pieces))
    factor = lax.rsqrt(mean + EPSILON)
    for d, piece in enumerate(pieces):
        at = pl.ds(pl.multiple_of(rot_ref[d] * width, 128), width)
        v = piece[...]
        hid_ref[:, at] = v
        normed_ref[:, at] = (v.astype(F32) * factor * gain_ref[:, at]).astype(BF16)


def join_kernel(rot_ref, live_ref, *refs):
    pieces, out_ref = refs[:-1], refs[-1]
    width = pieces[0].shape[1]
    for d, piece in enumerate(pieces):
        at = pl.ds(pl.multiple_of(rot_ref[d] * width, 128), width)
        out_ref[:, at] = (piece[...].astype(F32) * live_ref[...]).astype(BF16)


def land_kernel(rot_ref, base_ref, live_ref, *refs):
    pieces, out_ref = refs[:-1], refs[-1]
    for d, piece in enumerate(pieces):

        @pl.when(pl.program_id(0) == d)
        def _(piece=piece):
            total = base_ref[...].astype(F32) + live_ref[...] * piece[...].astype(F32)
            out_ref[...] = total.astype(out_ref.dtype)


def swap(v, bit, count):
    return lax.ppermute(v, "dp", [(i, i ^ (1 << bit)) for i in range(count)])


def rotate(v, by, count):
    return lax.ppermute(v, "tensor", [(i, (i + by) % count) for i in range(count)])


def in_order(pieces, column):
    return jnp.roll(jnp.stack([pieces[0]] + pieces[:0:-1]), column, axis=0)


def gather_pieces(v, count):
    bits = count.bit_length() - 1
    if bits == 3:
        near, far = swap(v, 1, count), swap(v, 2, count)
        half = v.shape[1] // 2
        first = swap(near[:, :half], 2, count)
        second = swap(far[:, half:], 1, count)
        mine = [(v, 0, 0), (near, 2, 0), (far, 4, 0), (first, 6, 0), (second, 6, half)]
    else:
        mine = [(v, 0, 0)]
        for bit in range(1, bits):
            mine += [(swap(a, bit, count), m ^ (1 << bit), o) for a, m, o in mine]
    return mine + [(swap(a, 0, count), m ^ 1, o) for a, m, o in mine]


def reduce_core(keep, received):
    return keep + received.astype(F32)


def scatter_rows(total, count, index):
    bits = count.bit_length() - 1
    q = index >> 1
    def run(v, order):
        left = list(range(1, bits))
        for bit in order:
            place_of = left.index(bit)
            low = 1 << place_of
            shaped = v.reshape((v.shape[0] // (2 * low), 2, low) + v.shape[1:])
            mine = (q >> (bit - 1)) & 1
            sent = lax.dynamic_index_in_dim(shaped, 1 - mine, 1, keepdims=False).astype(BF16)
            kept = lax.dynamic_index_in_dim(shaped, mine, 1, keepdims=False).astype(F32)
            v = (kept + swap(sent, bit, count).astype(F32)).reshape(
                (v.shape[0] // 2,) + v.shape[1:]
            )
            left.remove(bit)
        return v[0]

    order = list(range(1, bits))
    half = total.shape[2] // 2
    half = half - half % 128
    return jnp.concatenate(
        [run(total[:, :, :half], order), run(total[:, :, half:], order[::-1])], axis=1
    )


def pair_lanes(v):
    wide = jnp.pad(v, ((0, 0), (0, 64 - v.shape[1])))
    return jnp.concatenate([wide, wide], axis=1)


def local(
    dp_count, tensor_count,
    hidden_in, out_grad, seq_lengths, seq_device, seq_offset, norm_gain, w_gate, w_input, w_shared,
    w_step, conv_inner, conv_shared, conv_inner_bias, conv_shared_bias, step_bias, decay_log,
    skip_gain, gate_norm_gain, w_output,
):
    parts = tensor_count
    dp = lax.axis_index("dp")
    column = lax.axis_index("tensor")
    core, q = dp & 1, dp >> 1
    rows_dev, piece = hidden_in.shape
    rows = rows_dev // parts
    blocks = rows // LEN
    model = norm_gain.shape[0]
    shard = w_input.shape[1]
    inner = shard * parts
    heads_shard = w_step.shape[1]
    heads = heads_shard * parts
    width = inner // heads
    nstate = w_shared.shape[1] // 2
    groups = dp_count // 2

    aligned = piece % 128 == 0
    turn = jnp.stack([(column - d) % parts for d in range(parts)]).astype(jnp.int32)

    def send_rows(v, halo):
        pieces = []
        for d in range(parts):
            start = (column + d) % parts * rows
            mine = lax.dynamic_slice_in_dim(v, start, rows, 0)
            if halo:
                before = lax.dynamic_slice_in_dim(v, jnp.maximum(start - HALO, 0), HALO, 0)
                mine = jnp.concatenate([mine, before], axis=0)
            pieces.append(rotate(mine, d, parts) if d else mine)
        return pieces

    def send_back(v):
        pieces = []
        for d in range(parts):
            mine = lax.dynamic_slice_in_dim(v, (column + d) % parts * piece, piece, 1)
            pieces.append(rotate(mine, d, parts) if d else mine)
        return pieces

    def land(pieces, base, live_rows, dtype):
        if not aligned:
            total = in_order(pieces, column).reshape(rows_dev, piece).astype(F32)
            return (base.astype(F32) + live_rows * total).astype(dtype)
        return pl.pallas_call(
            land_kernel,
            grid_spec=pltpu.PrefetchScalarGridSpec(
                num_scalar_prefetch=1,
                grid=(parts,),
                in_specs=[
                    pl.BlockSpec((rows, piece), lambda d, rot: (rot[d], 0)),
                    pl.BlockSpec((rows, 1), lambda d, rot: (rot[d], 0)),
                ]
                + [pl.BlockSpec((rows, piece), lambda d, rot: (0, 0))] * parts,
                out_specs=pl.BlockSpec((rows, piece), lambda d, rot: (rot[d], 0)),
            ),
            out_shape=jax.ShapeDtypeStruct((rows_dev, piece), dtype),
            compiler_params=pltpu.CompilerParams(vmem_limit_bytes=VMEM),
            cost_estimate=pl.CostEstimate(
                flops=0, bytes_accessed=rows_dev * piece * 10, transcendentals=0
            ),
            name="land",
        )(turn, base, live_rows, *pieces)

    def row_block(size):
        return max(n for n in range(16, 129, 16) if size % n == 0)

    def join(kernel, pieces, extra, extra_rows, outs):
        size = pieces[0].shape[0]
        block = row_block(size)
        extra_spec = (
            pl.BlockSpec((block, 1), lambda g, rot: (g, 0))
            if extra_rows
            else pl.BlockSpec(extra.shape, lambda g, rot: (0, 0))
        )
        wide = pl.BlockSpec((block, model), lambda g, rot: (g, 0))
        return pl.pallas_call(
            kernel,
            grid_spec=pltpu.PrefetchScalarGridSpec(
                num_scalar_prefetch=1,
                grid=(size // block,),
                in_specs=[extra_spec]
                + [pl.BlockSpec((block, piece), lambda g, rot: (g, 0))] * parts,
                out_specs=[wide] * outs,
            ),
            out_shape=[jax.ShapeDtypeStruct((size, model), BF16)] * outs,
            compiler_params=pltpu.CompilerParams(vmem_limit_bytes=VMEM),
            cost_estimate=pl.CostEstimate(
                flops=0, bytes_accessed=size * model * 2 * (1 + outs), transcendentals=0
            ),
            name="join",
        )(turn, extra, *pieces)

    def join_plain(pieces):
        ordered = in_order(pieces, column)
        return jnp.concatenate([ordered[t] for t in range(parts)], axis=1)

    k_rows = model // dp_count
    place_dp = core * (model // 2) + q * k_rows

    def spread_out(v):
        return jnp.stack([v] + [rotate(v, d, parts) for d in range(1, parts)])

    def slices_of(index):
        other_core, other_q = index & 1, index >> 1
        return other_core, other_q

    def gather_columns(w):
        mine = lax.dynamic_slice_in_dim(w, place_dp, k_rows, 0)
        pieces = gather_pieces(spread_out(mine), dp_count)
        rows_of, cols_of = [], []
        for _, mask, offset in pieces:
            c2, q2 = slices_of(dp ^ mask)
            rows_of.append([c2 * (model // 2) + q2 * k_rows + offset] * parts)
            cols_of.append([turn[d] * shard for d in range(parts)])
        return place([a for a, _, _ in pieces], rows_of, cols_of, (model, inner))

    out_rows = shard // dp_count

    def gather_output(w):
        if out_rows % 16:
            return lax.all_gather(w, "tensor", axis=0, tiled=True)
        mine = lax.dynamic_slice_in_dim(w, core * (shard // 2) + q * out_rows, out_rows, 0)
        pieces = gather_pieces(spread_out(mine), dp_count)
        rows_of = []
        for _, mask, offset in pieces:
            c2, q2 = slices_of(dp ^ mask)
            start = c2 * (shard // 2) + q2 * out_rows + offset
            rows_of.append([turn[d] * shard + start for d in range(parts)])
        return place([a for a, _, _ in pieces], rows_of, None, (inner, model))

    hid_pieces = send_rows(hidden_in, True)
    w_in = gather_columns(w_input)

    small = jnp.concatenate(
        [
            conv_inner.reshape(-1),
            conv_inner_bias,
            gate_norm_gain,
            step_bias,
            decay_log,
            skip_gain,
            w_step.astype(F32).reshape(-1),
        ]
    )
    small = in_order([small] + [rotate(small, d, parts) for d in range(1, parts)], column)
    bounds = [0]
    for size in (4 * shard, shard, shard, heads_shard, heads_shard, heads_shard, model * heads_shard):
        bounds.append(bounds[-1] + size)
    take = lambda i: small[:, bounds[i] : bounds[i + 1]]
    taps = jnp.swapaxes(take(0).reshape(parts, 4, shard), 0, 1).reshape(4, inner)
    inner_bias = take(1).reshape(1, inner)
    gain_out = take(2).reshape(1, inner)
    steps_bias = take(3).reshape(1, heads)
    logs = take(4).reshape(1, heads)
    skips = take(5).reshape(1, heads)
    w_steps = (
        jnp.swapaxes(take(6).reshape(parts, model, heads_shard), 0, 1)
        .reshape(model, heads)
        .astype(BF16)
    )
    skip_wide = jnp.repeat(skips, width, axis=1)

    block_start = column * rows + jnp.arange(blocks + 1, dtype=jnp.int32) * LEN
    inside = (
        (seq_device[None, :] == dp)
        & (block_start[:, None] >= seq_offset[None, :])
        & (block_start[:, None] < seq_offset[None, :] + seq_lengths[None, :])
    )
    offset = jnp.sum(jnp.where(inside, block_start[:, None] - seq_offset[None, :], 0), axis=1)
    keep = (offset > 0).astype(jnp.int32)
    keep_f = keep.astype(F32)
    live_blocks = jnp.sum(inside.astype(F32), axis=1)[:blocks]
    live = jnp.repeat(live_blocks, LEN)[:, None]
    dev_start = jnp.arange(rows_dev // LEN, dtype=jnp.int32) * LEN
    dev_inside = (
        (seq_device[None, :] == dp)
        & (dev_start[:, None] >= seq_offset[None, :])
        & (dev_start[:, None] < seq_offset[None, :] + seq_lengths[None, :])
    )
    live_dev = jnp.repeat(jnp.sum(dev_inside.astype(F32), axis=1), LEN)[:, None]

    lane_head = jnp.arange(inner, dtype=jnp.int32) // width
    half_index = jnp.arange(128, dtype=jnp.int32) % 64
    spread = (half_index[:, None] == lane_head[None, :]).astype(BF16)
    select = (lane_head[:, None] == jnp.arange(128, dtype=jnp.int32)[None, :]).astype(BF16)
    columns = (
        (jnp.arange(192, dtype=jnp.int32) % 64)[:, None]
        == (jnp.arange(heads * LEN, dtype=jnp.int32) // LEN)[None, :]
    ).astype(BF16)

    if aligned:
        hid, normed_all = join(norm_kernel, hid_pieces, norm_gain[None, :], False, 2)
    else:
        hid = join_plain(hid_pieces)
        wide_in = hid.astype(F32)
        mean = jnp.mean(wide_in * wide_in, axis=1, keepdims=True)
        normed_all = (wide_in * lax.rsqrt(mean + EPSILON) * norm_gain[None, :]).astype(BF16)
    normed = normed_all[:rows]
    w_misc = jnp.concatenate(
        [w_shared, w_steps, jnp.zeros((model, 128 - heads), BF16)], axis=1
    )
    misc = dot_nn(normed_all, w_misc)
    inner_proj = dot_nn(normed_all, w_in)

    shared_all = misc[:, : 2 * nstate]
    shared_ext = jnp.concatenate([shared_all[rows + 8 :], shared_all[:rows]], axis=0)
    row_in_block = jnp.arange(rows + 8, dtype=jnp.int32) % LEN
    starts = jnp.repeat(1.0 - keep_f, LEN)[: rows + 8]

    def allowed(lag):
        return (1.0 - starts * (row_in_block < lag).astype(F32))[:, None]

    shared_u = conv_shared_bias[None, :] + conv_shared[3][None, :] * shared_ext[8:]
    for lag in range(1, 4):
        shared_u = shared_u + conv_shared[3 - lag][None, :] * (
            shared_ext[8 - lag : 8 - lag + rows] * allowed(lag)[:rows]
        )
    shared_open = jax.nn.sigmoid(shared_u)
    shared_conv = shared_u * shared_open
    b_map, c_map = shared_conv[:, :nstate], shared_conv[:, nstate:]

    raw = misc[:rows, 2 * nstate : 2 * nstate + heads] + steps_bias
    delta = jax.nn.softplus(raw)
    rates = jnp.exp(logs)
    decays = -delta * rates
    triangle = (jnp.arange(LEN)[:, None] >= jnp.arange(LEN)[None, :]).astype(F32)
    cum = jnp.einsum(
        "ts,csh->cth", triangle, decays.reshape(blocks, LEN, heads), precision=PRECISE
    )
    last = cum[:, -1, :]
    fall = jnp.exp(last[:, None, :] - cum).reshape(rows, heads)
    dec = jnp.exp(last)
    cum = cum.reshape(rows, heads)
    cum_t = cum.T
    padded = jnp.pad(cum, ((0, 0), (0, 64 - heads)))
    cum3 = jnp.concatenate([padded] * 3, axis=1)
    delta2 = pair_lanes(delta)
    grow2 = pair_lanes(jnp.exp(cum))
    fall2 = pair_lanes(fall)
    coef2 = pair_lanes(fall * delta)
    pref = [jnp.ones((heads,), F32) * keep_f[0]]
    for c in range(1, blocks):
        pref.append(keep_f[c] * dec[c - 1] * pref[-1])
    through = jnp.repeat(dec[blocks - 1] * pref[-1], width)[None, :]
    pref_wide = jnp.repeat(jnp.stack(pref), width, axis=1)[:, None, :]
    dec_wide = jnp.repeat(dec, width, axis=1)[:, None, :]

    params = pltpu.CompilerParams(vmem_limit_bytes=VMEM)
    smem = pl.BlockSpec(memory_space=pltpu.SMEM)
    full = lambda *shape: pl.BlockSpec(shape, lambda g: (0,) * len(shape))
    up = lambda *shape: pl.BlockSpec(shape, lambda g: (g,) + (0,) * (len(shape) - 1))
    down = lambda *shape: pl.BlockSpec(
        shape, lambda g: (blocks - 1 - g,) + (0,) * (len(shape) - 1)
    )
    out = jax.ShapeDtypeStruct
    cost = lambda flops, size: pl.CostEstimate(
        flops=flops, bytes_accessed=size, transcendentals=rows * inner
    )
    halo_block = pl.BlockSpec((HALO, inner), lambda g: (rows // HALO, 0))
    wide_map = 2 * rows * inner * nstate

    u, local_states, chunk_state = pl.pallas_call(
        conv_states_kernel,
        grid=(blocks,),
        in_specs=[
            smem, up(LEN, inner), halo_block, full(4, inner), full(1, inner), up(LEN, nstate),
            up(LEN, 128), up(1, 1, inner), full(128, inner),
        ],
        out_specs=[up(LEN, inner), up(1, nstate, inner), full(nstate, inner)],
        out_shape=[
            out((rows, inner), F32), out((blocks, nstate, inner), BF16), out((nstate, inner), F32),
        ],
        scratch_shapes=[pltpu.VMEM((LEN + 8, inner), F32), pltpu.VMEM((nstate, inner), F32)],
        compiler_params=params,
        cost_estimate=cost(2 * wide_map, rows * inner * 12),
        name="conv_states",
    )(keep, inner_proj, inner_proj, taps, inner_bias, b_map, coef2, dec_wide, spread)

    to_right = [(i, i + 1) for i in range(parts - 1)]
    to_left = [(i + 1, i) for i in range(parts - 1)]
    entering = lax.ppermute(chunk_state.astype(BF16), "tensor", to_right)
    for _ in range(parts - 2):
        entering = lax.ppermute(
            (chunk_state + through * entering.astype(F32)).astype(BF16), "tensor", to_right
        )

    y_within = pl.pallas_call(
        within_kernel,
        grid=(blocks,),
        in_specs=[
            up(LEN, inner), up(LEN, 192), pl.BlockSpec((heads, LEN), lambda g: (0, g)),
            up(LEN, 128), up(LEN, nstate), up(LEN, nstate), full(192, heads * LEN),
            full(128, inner),
        ],
        out_specs=up(LEN, inner),
        out_shape=out((rows, inner), F32),
        compiler_params=params,
        cost_estimate=cost(8 * wide_map, rows * inner * 8),
        name="within",
    )(u, cum3, cum_t, delta2, b_map, c_map, columns, spread)

    w_gates = gather_columns(w_gate)
    w_out = gather_output(w_output)
    grad_pieces = send_rows(out_grad, False)
    if aligned:
        (masked,) = join(join_kernel, grad_pieces, live, True, 1)
    else:
        masked = join_plain(grad_pieces) * live.astype(BF16)
    gate_proj = dot_nn(normed, w_gates)
    normed_y_grad = dot_nt(masked, w_out)

    normed_y, scan_grad, gate_grad, q_plus, dc_across, gain_out_grad, skip_lanes, chunk_grad = (
        pl.pallas_call(
            gate_kernel,
            grid=(blocks,),
            in_specs=[
                smem, down(LEN, inner), down(LEN, inner), down(LEN, inner), down(LEN, inner),
                down(1, nstate, inner), full(nstate, inner), down(1, 1, inner), down(LEN, nstate),
                down(LEN, 128), full(1, inner), full(1, inner), down(1, 1, inner),
                full(128, inner), full(inner, 128),
            ],
            out_specs=[
                down(LEN, inner), down(LEN, inner), down(LEN, inner), down(LEN, 128),
                down(LEN, nstate), full(1, inner), full(1, inner), full(nstate, inner),
            ],
            out_shape=[
                out((rows, inner), BF16), out((rows, inner), BF16), out((rows, inner), BF16),
                out((rows, 128), F32), out((rows, nstate), F32), out((1, inner), F32),
                out((1, inner), F32), out((nstate, inner), F32),
            ],
            scratch_shapes=[
                pltpu.VMEM((LEN, inner), F32), pltpu.VMEM((nstate, inner), BF16),
                pltpu.VMEM((nstate, inner), F32),
            ],
            compiler_params=params,
            cost_estimate=cost(6 * wide_map, rows * inner * 24),
            name="gate",
        )(
            keep, y_within, u, gate_proj, normed_y_grad, local_states, entering, pref_wide, c_map,
            grow2, skip_wide, gain_out, dec_wide, spread, select,
        )
    )

    leaving = lax.ppermute(chunk_grad.astype(BF16), "tensor", to_left)
    for _ in range(parts - 2):
        leaving = lax.ppermute(
            (chunk_grad + through * leaving.astype(F32)).astype(BF16), "tensor", to_left
        )

    mixed_rows = dot_nn(normed_y, w_out).astype(BF16)

    mixed_out = land(send_back(mixed_rows), hidden_in, live_dev, BF16)

    def half_of(v, which):
        size = v.shape[1] // 2
        return lax.dynamic_slice_in_dim(v, which * size, size, 1)

    def finish(part_of, extra):
        pieces = []
        for d in range(parts):
            mine = part_of((column + d) % parts)
            if extra is not None:
                mine = jnp.concatenate([mine, extra], axis=1)
            mine = mine.astype(BF16)
            pieces.append(rotate(mine, d, parts) if d else mine)
        total = jnp.sum(in_order(pieces, column).astype(F32), axis=0).astype(BF16)
        return gather_pieces(total[None], dp_count)

    def column_grads(grads, extra_width):
        sent = swap(dot_tn(half_of(normed, 1 - core), grads).astype(BF16), 0, dp_count)
        total = reduce_core(dot_tn(half_of(normed, core), grads), sent)
        total = scatter_rows(total.reshape(groups, k_rows, -1), dp_count, dp)
        pieces = finish(
            lambda t: lax.dynamic_slice_in_dim(total, t * shard, shard, 1),
            total[:, inner:] if extra_width else None,
        )
        rows_of = []
        for _, mask, at in pieces:
            c2, q2 = slices_of(dp ^ mask)
            rows_of.append([c2 * (model // 2) + q2 * k_rows + at])
        return place(
            [a for a, _, _ in pieces], rows_of, None, (model, shard + extra_width)
        ).astype(F32)

    def output_grads():
        sent = swap(dot_tn(normed_y, half_of(masked, 1 - core)).astype(BF16), 0, dp_count)
        total = reduce_core(dot_tn(normed_y, half_of(masked, core)), sent)
        cols = model // 2
        size = shard // groups
        total = total.reshape(parts, groups, size, cols)
        total = jnp.swapaxes(total, 0, 1).reshape(groups, parts * size, cols)
        total = scatter_rows(total, dp_count, dp).reshape(parts, size, cols)
        pieces = finish(lambda t: lax.dynamic_index_in_dim(total, t, 0, keepdims=False), None)
        rows_of, cols_of = [], []
        for _, mask, at in pieces:
            c2, q2 = slices_of(dp ^ mask)
            rows_of.append([q2 * size + at])
            cols_of.append([c2 * cols])
        return place([a for a, _, _ in pieces], rows_of, cols_of, (shard, model)).astype(F32)

    w_gate_grad = column_grads(gate_grad, 0)
    w_output_grad = output_grads()
    gate_part = dot_nt(gate_grad, w_gates)

    dv_within, db_within, dc_within = pl.pallas_call(
        within_back_kernel,
        grid=(blocks,),
        in_specs=[
            up(LEN, inner), up(LEN, inner), up(LEN, 192),
            pl.BlockSpec((heads, LEN), lambda g: (0, g)), up(LEN, 128), up(LEN, nstate),
            up(LEN, nstate), full(192, heads * LEN), full(128, inner),
        ],
        out_specs=[up(LEN, inner), up(LEN, nstate), up(LEN, nstate)],
        out_shape=[out((rows, inner), F32), out((rows, nstate), F32), out((rows, nstate), F32)],
        compiler_params=params,
        cost_estimate=cost(16 * wide_map, rows * inner * 10),
        name="within_back",
    )(u, scan_grad, cum3, cum_t, delta2, b_map, c_map, columns, spread)

    inner_grad, db_across, q_minus, step_sums, end_lanes, taps_grad, bias_grad, head_rows = (
        pl.pallas_call(
            across_back_kernel,
            grid=(blocks,),
            in_specs=[
                smem, down(LEN, inner), down(LEN, inner), down(LEN, inner), down(LEN, inner),
                halo_block, down(1, nstate, inner), full(nstate, inner), down(1, 1, inner),
                full(nstate, inner), down(LEN, nstate), down(LEN, nstate), down(LEN, 128),
                down(LEN, 128), down(LEN, 128), full(1, inner), down(1, 1, inner), full(4, inner),
                full(128, inner), full(inner, 128),
            ],
            out_specs=[
                down(LEN, inner), down(LEN, nstate), down(LEN, 128), down(LEN, 128),
                down(1, 1, inner), full(4, inner), full(1, inner), full(8, inner),
            ],
            out_shape=[
                out((rows, inner), BF16), out((rows, nstate), F32), out((rows, 128), F32),
                out((rows, 128), F32), out((blocks, 1, inner), F32), out((4, inner), F32),
                out((1, inner), F32), out((8, inner), F32),
            ],
            scratch_shapes=[
                pltpu.VMEM((nstate, inner), F32), pltpu.VMEM((LEN + 8, inner), F32),
            ],
            compiler_params=params,
            cost_estimate=cost(6 * wide_map, rows * inner * 20),
            name="across_back",
        )(
            keep, u, scan_grad, dv_within, inner_proj, inner_proj, local_states, entering,
            pref_wide, leaving, b_map, c_map, grow2, fall2, delta2, skip_wide, dec_wide, taps,
            spread, select,
        )
    )

    shared_du = jnp.concatenate([db_within + db_across, dc_within + dc_across], axis=1) * (
        shared_open * (1.0 + shared_u * (1.0 - shared_open))
    )
    heads_of_chunk = lax.ppermute(
        jnp.concatenate([head_rows, shared_du[:8] * keep_f[0]], axis=1), "tensor", to_left
    )
    tail = inner_grad[rows - 16 :].astype(F32)
    later = jnp.concatenate([jnp.zeros((8, inner), F32), heads_of_chunk[:, :inner]], axis=0)
    for lag in range(1, 4):
        moved = jnp.concatenate(
            [jnp.zeros((16 - lag, inner), F32), heads_of_chunk[:lag, :inner]], axis=0
        )
        tail = tail + taps[3 - lag][None, :] * moved
    inner_grad = lax.dynamic_update_slice(inner_grad, tail.astype(BF16), (rows - 16, 0))

    shared_later = jnp.concatenate([shared_du, heads_of_chunk[:, inner:]], axis=0)
    shared_grad = conv_shared[3][None, :] * shared_du
    conv_shared_grad = [None] * 4
    conv_shared_grad[3] = jnp.sum(shared_du * shared_ext[8:], axis=0)
    for lag in range(1, 4):
        blocked = (shared_later * allowed(lag))[lag : lag + rows]
        shared_grad = shared_grad + conv_shared[3 - lag][None, :] * blocked
        conv_shared_grad[3 - lag] = jnp.sum(
            shared_du * shared_ext[8 - lag : 8 - lag + rows] * allowed(lag)[:rows], axis=0
        )
    shared_grad = shared_grad.astype(BF16)
    conv_shared_grad = jnp.stack(conv_shared_grad)
    conv_shared_bias_grad = jnp.sum(shared_du, axis=0)

    ends = jnp.sum(end_lanes.reshape(blocks, heads, width), axis=2)
    dcum = (q_plus - q_minus)[:, :heads].reshape(blocks, LEN, heads)
    da = (
        jnp.einsum("ts,cth->csh", triangle, dcum, precision=PRECISE) + ends[:, None, :]
    ).reshape(rows, heads)
    raw_grad = (step_sums[:, :heads] - da * rates) * jax.nn.sigmoid(raw)
    step_grad = raw_grad.astype(BF16)
    decay_log_grad = jnp.sum(da * decays, axis=0)
    step_bias_grad = jnp.sum(raw_grad, axis=0)
    skip_gain_grad = jnp.sum(skip_lanes.reshape(heads, width), axis=1)

    misc_grad = jnp.concatenate(
        [shared_grad, step_grad, jnp.zeros((rows, 128 - heads), BF16)], axis=1
    )
    w_in_grad = column_grads(
        jnp.concatenate([inner_grad, misc_grad], axis=1), 2 * nstate + 128
    )
    normed_grad = gate_part + dot_nt(inner_grad, w_in) + dot_nt(misc_grad, w_misc)
    own = hid[:rows].astype(F32)
    own_factor = lax.rsqrt(jnp.mean(own * own, axis=1, keepdims=True) + EPSILON)
    weighted = normed_grad * norm_gain[None, :]
    row_stat = jnp.sum(weighted * own, axis=1, keepdims=True)
    input_grad = (
        own_factor * weighted
        - own * (own_factor * own_factor * own_factor * row_stat / model)
    ).astype(BF16)
    norm_gain_grad = jnp.sum(normed_grad * own * own_factor, axis=0)
    hidden_grad = land(send_back(input_grad), out_grad, live_dev, F32)

    tiny = jnp.concatenate(
        [
            taps_grad.reshape(-1), bias_grad.reshape(-1), gain_out_grad.reshape(-1),
            step_bias_grad, decay_log_grad, skip_gain_grad, conv_shared_grad.reshape(-1),
            conv_shared_bias_grad, norm_gain_grad,
        ]
    )
    for bit in range(dp_count.bit_length() - 1):
        tiny = tiny + swap(tiny, bit, dp_count)
    tiny = jnp.sum(
        in_order([tiny] + [rotate(tiny, d, parts) for d in range(1, parts)], column), axis=0
    )
    ends_at = [0]
    for size in (4 * inner, inner, inner, heads, heads, heads, 8 * nstate, 2 * nstate, model):
        ends_at.append(ends_at[-1] + size)
    part = lambda i: tiny[ends_at[i] : ends_at[i + 1]]
    own_part = lambda v, size: lax.dynamic_slice_in_dim(v, column * size, size, 0)
    conv_inner_grad = lax.dynamic_slice_in_dim(part(0).reshape(4, inner), column * shard, shard, 1)
    w_step_grad = lax.dynamic_slice_in_dim(
        w_in_grad, shard + 2 * nstate + column * heads_shard, heads_shard, 1
    )
    return (
        mixed_out,
        hidden_grad,
        part(8),
        w_gate_grad,
        w_in_grad[:, :shard],
        w_in_grad[:, shard : shard + 2 * nstate],
        w_step_grad,
        conv_inner_grad,
        part(6).reshape(4, 2 * nstate),
        own_part(part(1), shard),
        part(7),
        own_part(part(3), heads_shard),
        own_part(part(4), heads_shard),
        own_part(part(5), heads_shard),
        own_part(part(2), shard),
        w_output_grad,
    )


def solution(mesh):
    split = P("tensor")
    in_specs = (
        P("dp", "tensor"), P("dp", "tensor"), P(), P(), P(), P(), P(None, "tensor"),
        P(None, "tensor"), P(), P(None, "tensor"), P(None, "tensor"), P(), split, P(), split,
        split, split, split, P("tensor", None),
    )
    out_specs = (
        P("dp", "tensor"), P("dp", "tensor"), P(), P(None, "tensor"), P(None, "tensor"), P(),
        P(None, "tensor"), P(None, "tensor"), P(), split, P(), split, split, split, split,
        P("tensor", None),
    )
    body = functools.partial(local, mesh.shape["dp"], mesh.shape["tensor"])
    return jax.shard_map(body, mesh=mesh, in_specs=in_specs, out_specs=out_specs, check_vma=False)
```

```python
import functools

import jax
import jax.numpy as jnp
from jax import lax
from jax.experimental import pallas as pl
from jax.experimental.pallas import tpu as pltpu
from jax.sharding import PartitionSpec as P

F32 = jnp.float32
BF16 = jnp.bfloat16
PRECISE = lax.Precision.HIGHEST
EPSILON = 1e-05
LEN = 128
HALO = 16
WIDE = 256
VMEM = 52 * 1024 * 1024


def dot_nn(a, b):
    return jnp.dot(a, b, preferred_element_type=F32)


def dot_nt(a, b):
    return lax.dot_general(a, b, (((1,), (1,)), ((), ())), preferred_element_type=F32)


def dot_tn(a, b):
    return lax.dot_general(a, b, (((0,), (0,)), ((), ())), preferred_element_type=F32)


def sigmoid(v):
    return 0.5 * jnp.tanh(0.5 * v) + 0.5


def split_pair(v):
    lane = lax.broadcasted_iota(jnp.int32, v.shape, 1)
    high = v.astype(BF16).astype(F32)
    return jnp.where(lane < 64, high, v - high).astype(BF16)


def split_triple(v):
    lane = lax.broadcasted_iota(jnp.int32, v.shape, 1)
    high = v.astype(BF16).astype(F32)
    rest = v - high
    middle = rest.astype(BF16).astype(F32)
    return jnp.where(lane < 64, high, jnp.where(lane < 128, middle, rest - middle)).astype(BF16)


def head_sums(v, select):
    high = v.astype(BF16)
    low = (v - high.astype(F32)).astype(BF16)
    return dot_nn(high, select) + dot_nn(low, select)


def halves(v):
    high = v.astype(BF16)
    return high, (v - high.astype(F32)).astype(BF16)


def finer(dot, a, b):
    a_high, a_low = halves(a)
    b_high, b_low = halves(b)
    return dot(a_high, b_high) + (dot(a_high, b_low) + dot(a_low, b_high))


def fold(v):
    total = v[:, :128]
    for i in range(1, v.shape[1] // 128):
        total = total + v[:, i * 128 : (i + 1) * 128]
    return total


def chunk(i, width):
    return pl.ds(pl.multiple_of(i * width, width), width)


def maps_kernel(
    keep_ref, misc_ref, halo_ref, taps_ref, bias_ref, step_bias_ref, logs_ref,
    u_ref, b_ref, c_ref, step_ref, slope_ref, rate_ref, cum_ref, cum_t_ref, grow_ref, fall_ref,
    coef_ref, dec_ref, ext_ref,
):
    c = pl.program_id(0)
    keep = keep_ref[c].astype(F32)
    shared = u_ref.shape[1]

    @pl.when(c == 0)
    def _():
        ext_ref[0:8, :] = halo_ref[8:16, :shared] * keep

    @pl.when(c > 0)
    def _():
        ext_ref[0:8, :] = ext_ref[LEN : LEN + 8, :] * keep

    ext_ref[8 : LEN + 8, :] = misc_ref[:, :shared]
    u = bias_ref[...] + taps_ref[3:4, :] * ext_ref[8 : 8 + LEN, :]
    for lag in range(1, 4):
        u = u + taps_ref[3 - lag : 4 - lag, :] * ext_ref[8 - lag : 8 - lag + LEN, :]
    u_ref[...] = u
    maps = u * sigmoid(u)
    b_ref[...] = maps[:, : shared // 2]
    c_ref[...] = maps[:, shared // 2 :]

    raw = misc_ref[:, shared:] + step_bias_ref[...]
    step = jnp.maximum(raw, 0.0) + jnp.log1p(jnp.exp(-jnp.abs(raw)))
    slope_ref[...] = sigmoid(raw)
    step_ref[...] = step
    rates = -step * jnp.exp(logs_ref[...])
    rate_ref[...] = rates
    cum = running_sum(rates, False)
    cum_ref[...] = jnp.concatenate([cum, cum[:, :64]], axis=1)
    cum_t_ref[...] = cum.T
    last = cum[LEN - 1 : LEN, :]
    fall = jnp.exp(last - cum)
    grow_ref[...] = jnp.exp(cum)
    fall_ref[...] = fall
    coef_ref[...] = fall * step
    dec_ref[0] = jnp.exp(last)


def running_sum(v, backwards):
    row = lax.broadcasted_iota(jnp.int32, (LEN, LEN), 0)
    col = lax.broadcasted_iota(jnp.int32, (LEN, LEN), 1)
    ones = jnp.where((row <= col) if backwards else (row >= col), 1.0, 0.0).astype(BF16)
    total = jnp.zeros(v.shape, F32)
    for _ in range(3):
        term = v.astype(BF16)
        total = total + dot_nn(ones, term)
        v = v - term.astype(F32)
    return total


def maps_back_kernel(
    keep_ref, db1_ref, db2_ref, dc1_ref, dc2_ref, u_ref, misc_ref, halo_ref, taps_ref, plus_ref,
    minus_ref, sums_ref, ends_ref, slope_ref, rate_ref, logs_ref, whole_ref,
    grad_ref, taps_grad_ref, bias_grad_ref, head_ref, vector_ref, ext_ref,
):
    g = pl.program_id(0)
    c = pl.num_programs(0) - 1 - g
    keep = keep_ref[c].astype(F32)
    shared = u_ref.shape[1]

    @pl.when(g == 0)
    def _():
        taps_grad_ref[...] = jnp.zeros_like(taps_grad_ref)
        bias_grad_ref[...] = jnp.zeros_like(bias_grad_ref)
        vector_ref[...] = jnp.zeros_like(vector_ref)
        ext_ref[LEN : LEN + 8, :] = jnp.zeros((8, shared), F32)

    @pl.when(g > 0)
    def _():
        ext_ref[LEN : LEN + 8, :] = ext_ref[0:8, :] * keep_ref[c + 1].astype(F32)

    u = u_ref[...]
    open_ = sigmoid(u)
    dmaps = jnp.concatenate([db1_ref[...] + db2_ref[...], dc1_ref[...] + dc2_ref[...]], axis=1)
    du = dmaps * (open_ * (1.0 + u * (1.0 - open_)))
    ext_ref[0:LEN, :] = du
    proj = misc_ref[:, :shared]
    bias_grad_ref[...] += jnp.sum(du, axis=0, keepdims=True)
    total = taps_ref[3:4, :] * du
    taps_grad_ref[3:4, :] += jnp.sum(proj * du, axis=0, keepdims=True)
    for lag in range(1, 4):
        later = ext_ref[lag : lag + LEN, :]
        total = total + taps_ref[3 - lag : 4 - lag, :] * later
        taps_grad_ref[3 - lag : 4 - lag, :] += jnp.sum(proj * later, axis=0, keepdims=True)
    da = running_sum(plus_ref[...] - minus_ref[...], True) + ends_ref[0, 0:1, :]
    raw_grad = (sums_ref[...] - da * jnp.exp(logs_ref[...])) * slope_ref[...]
    grad_ref[...] = jnp.concatenate([total, raw_grad], axis=1).astype(BF16)
    vector_ref[0:1, :] += jnp.sum(raw_grad, axis=0, keepdims=True)
    vector_ref[1:2, :] += jnp.sum(da * rate_ref[...], axis=0, keepdims=True)

    @pl.when(c == 0)
    def _():
        head_ref[...] = ext_ref[0:8, :] * keep
        for lag in range(1, 4):
            part = keep * ext_ref[0:lag, :] * halo_ref[HALO - lag : HALO, :shared]
            taps_grad_ref[3 - lag : 4 - lag, :] += jnp.sum(part, axis=0, keepdims=True)


def input_grad_kernel(ng_ref, hid_ref, gain_ref, out_ref, gain_grad_ref):
    @pl.when(pl.program_id(0) == 0)
    def _():
        gain_grad_ref[...] = jnp.zeros_like(gain_grad_ref)

    width = ng_ref.shape[1]
    u = hid_ref[...].astype(F32)
    ng = ng_ref[...]
    factor = lax.rsqrt(jnp.sum(fold(u * u), axis=1, keepdims=True) / width + EPSILON)
    gain_grad_ref[...] += jnp.sum(ng * u * factor, axis=0, keepdims=True)
    weighted = ng * gain_ref[...]
    stat = jnp.sum(fold(weighted * u), axis=1, keepdims=True) / width
    out_ref[...] = (factor * weighted - u * (factor * factor * factor * stat)).astype(BF16)


def conv_states_kernel(
    keep_ref, ip_ref, halo_ref, taps_ref, bias_ref, b_ref, coef_ref, dec_ref, spread_ref,
    u_ref, local_ref, out_ref, wide_ref, pref_ref, through_ref, ext_ref, state_ref, run_ref,
):
    c = pl.program_id(0)
    keep = keep_ref[c].astype(F32)

    @pl.when(c == 0)
    def _():
        state_ref[...] = jnp.zeros_like(state_ref)
        run_ref[...] = jnp.ones_like(run_ref)
        ext_ref[0:8, :] = halo_ref[8:16, :] * keep

    @pl.when(c > 0)
    def _():
        ext_ref[0:8, :] = ext_ref[LEN : LEN + 8, :] * keep

    ext_ref[8 : LEN + 8, :] = ip_ref[...]
    coef = split_pair(coef_ref[...])
    dec = split_pair(jnp.broadcast_to(dec_ref[0], (8, 128)))
    b_map, b_low = halves(b_ref[...])

    def step(i, carry):
        at = chunk(i, WIDE)
        u = bias_ref[:, at] + taps_ref[3:4, at] * ext_ref[8 : 8 + LEN, at]
        for lag in range(1, 4):
            u = u + taps_ref[3 - lag : 4 - lag, at] * ext_ref[8 - lag : 8 - lag + LEN, at]
        u_ref[:, at] = u
        spread = spread_ref[:, at]
        w = (u * sigmoid(u) * dot_nn(coef, spread)).astype(BF16)
        state = state_ref[:, at] * keep
        local_ref[0, :, at] = state.astype(BF16)
        decay = dot_nn(dec, spread)[0:1, :]
        wide_ref[0, :, at] = decay
        pref = run_ref[:, at] * keep
        pref_ref[0, :, at] = pref
        run_ref[:, at] = pref * decay
        state_ref[:, at] = decay * state + (dot_tn(b_map, w) + dot_tn(b_low, w))
        return carry

    lax.fori_loop(0, u_ref.shape[1] // WIDE, step, 0, unroll=3)

    @pl.when(c == pl.num_programs(0) - 1)
    def _():
        out_ref[...] = state_ref[...]
        through_ref[...] = run_ref[...]


def within_kernel(
    u_ref, cum_ref, cum_t_ref, step_ref, b_ref, c_ref, columns_ref, spread_ref, y_ref
):
    scores = finer(dot_nt, c_ref[...], b_ref[...])
    row = lax.broadcasted_iota(jnp.int32, (LEN, LEN), 0)
    col = lax.broadcasted_iota(jnp.int32, (LEN, LEN), 1)
    scores = jnp.where(row >= col, scores, 0.0)
    scores = jnp.concatenate([scores, scores], axis=1)
    cum = split_triple(cum_ref[...])
    steps = split_pair(step_ref[...])
    first = col < 64

    def pair(p, carry):
        at = chunk(p, 128)
        left = dot_nn(cum, columns_ref[:, chunk(p, 256)])
        right = jnp.concatenate(
            [cum_t_ref[pl.ds(2 * p, 1), :], cum_t_ref[pl.ds(2 * p + 1, 1), :]], axis=1
        )
        mixing = (jnp.exp(jnp.minimum(left - right, 0.0)) * scores).astype(BF16)
        u = u_ref[:, at]
        v = u * sigmoid(u) * dot_nn(steps, spread_ref[:, at])
        stacked = jnp.concatenate(
            [jnp.where(first, v, 0.0).astype(BF16), jnp.where(first, 0.0, v).astype(BF16)], axis=0
        )
        y_ref[:, at] = dot_nn(mixing, stacked)
        return carry

    lax.fori_loop(0, u_ref.shape[1] // 128, pair, 0, unroll=8)


def gate_kernel(
    keep_ref, y_ref, u_ref, gate_ref, ng_ref, local_ref, enter_ref, pref_ref, c_ref, grow_ref,
    skip_ref, gain_ref, dec_ref, spread_ref, select_ref,
    ny_ref, dy_ref, gg_ref, q_ref, dc_ref, gain_grad_ref, skip_grad_ref, out_ref,
    scan_ref, carried_ref, state_ref, high_ref, low_ref, z_ref,
):
    g = pl.program_id(0)
    c = pl.num_programs(0) - 1 - g
    width = y_ref.shape[1]
    keep = keep_ref[c].astype(F32)

    @pl.when(g == 0)
    def _():
        state_ref[...] = jnp.zeros_like(state_ref)
        gain_grad_ref[...] = jnp.zeros_like(gain_grad_ref)
        skip_grad_ref[...] = jnp.zeros_like(skip_grad_ref)

    c_map, c_low = halves(c_ref[...])
    grow = split_pair(grow_ref[...])

    def forward(i, sums):
        squares, stat = sums
        at = chunk(i, WIDE)
        carried = (
            local_ref[0, :, at].astype(F32) + pref_ref[0, :, at] * enter_ref[:, at].astype(F32)
        ).astype(BF16)
        carried_ref[:, at] = carried
        scanned = y_ref[:, at] + dot_nn(grow, spread_ref[:, at]) * (dot_nn(c_map, carried)+dot_nn(c_low,carried))
        scan_ref[:, at] = scanned
        u = u_ref[:, at]
        y = scanned + skip_ref[:, at] * (u * sigmoid(u))
        gate = gate_ref[:, at]
        gated = y * (gate * sigmoid(gate))
        squares = squares + fold(gated * gated)
        stat = stat + fold(ng_ref[:, at] * gain_ref[:, at] * gated)
        return (squares, stat)

    nothing = jnp.zeros((LEN, 128), F32)
    squares, stat = lax.fori_loop(0, width // WIDE, forward, (nothing, nothing), unroll=3)
    scale = lax.rsqrt(jnp.sum(squares, axis=1, keepdims=True) / width + EPSILON)
    back = scale * scale * scale * (jnp.sum(stat, axis=1, keepdims=True) / width)

    def backward(i, carry):
        at = chunk(i, WIDE)
        scanned = scan_ref[:, at]
        u = u_ref[:, at]
        x = u * sigmoid(u)
        y = scanned + skip_ref[:, at] * x
        gate = gate_ref[:, at]
        open_ = sigmoid(gate)
        act = gate * open_
        gated = y * act
        scaled = gated * scale
        ng = ng_ref[:, at]
        gain = gain_ref[:, at]
        ny_ref[:, at] = (scaled * gain).astype(BF16)
        gain_grad_ref[:, at] += jnp.sum(ng * scaled, axis=0, keepdims=True)
        gated_grad = scale * (ng * gain) - gated * back
        gg_ref[:, at] = (gated_grad * y * open_ * (1.0 + gate * (1.0 - open_))).astype(BF16)
        dy_low = (gated_grad * act).astype(BF16)
        dy_ref[:, at] = dy_low
        dy = dy_low.astype(F32)
        skip_grad_ref[:, at] += jnp.sum(dy * x, axis=0, keepdims=True)
        high_ref[:, at], low_ref[:, at] = halves(dy * scanned)
        z = (dot_nn(grow, spread_ref[:, at]) * dy).astype(BF16)
        z_ref[:, at] = z
        state_ref[:, at] = keep * (dec_ref[0, :, at] * state_ref[:, at] + (dot_tn(c_map, z)+dot_tn(c_low,z)))
        return carry

    lax.fori_loop(0, width // WIDE, backward, 0, unroll=3)
    select = select_ref[...]
    q_ref[...] = dot_nn(high_ref[...], select) + dot_nn(low_ref[...], select)
    dc_ref[...] = dot_nt(z_ref[...], carried_ref[...])

    @pl.when(c == 0)
    def _():
        out_ref[...] = state_ref[...]


def within_back_kernel(
    u_ref, dy_ref, cum_ref, cum_t_ref, step_ref, b_ref, c_ref, columns_ref, spread_ref,
    dv_ref, db_ref, dc_ref,
):
    scores = finer(dot_nt, b_ref[...], c_ref[...])
    row = lax.broadcasted_iota(jnp.int32, (LEN, LEN), 0)
    col = lax.broadcasted_iota(jnp.int32, (LEN, LEN), 1)
    scores = jnp.where(row <= col, scores, 0.0)
    scores = jnp.concatenate([scores, scores], axis=1)
    cum = split_triple(cum_ref[...])
    steps = split_pair(step_ref[...])
    first = col < 64

    def pair(p, total):
        at = chunk(p, 128)
        left = dot_nn(cum, columns_ref[:, chunk(p, 256)])
        right = jnp.concatenate(
            [cum_t_ref[pl.ds(2 * p, 1), :], cum_t_ref[pl.ds(2 * p + 1, 1), :]], axis=1
        )
        decay = jnp.exp(jnp.minimum(right - left, 0.0))
        mixing = (decay * scores).astype(BF16)
        dy_low = dy_ref[:, at]
        dy = dy_low.astype(F32)
        dy_stack = jnp.concatenate(
            [jnp.where(first, dy, 0.0).astype(BF16), jnp.where(first, 0.0, dy).astype(BF16)], axis=0
        )
        dv_ref[:, at] = dot_nn(mixing, dy_stack)
        u = u_ref[:, at]
        v = u * sigmoid(u) * dot_nn(steps, spread_ref[:, at])
        v_stack = jnp.concatenate(
            [jnp.where(first, v, 0.0).astype(BF16), jnp.where(first, 0.0, v).astype(BF16)], axis=0
        )
        dw = dot_nt(v_stack, dy_low)
        return total + decay[:, :LEN] * dw[:LEN] + decay[:, LEN:] * dw[LEN:]

    total = lax.fori_loop(
        0, u_ref.shape[1] // 128, pair, jnp.zeros((LEN, LEN), F32), unroll=8
    )
    total = jnp.where(row <= col, total, 0.0)
    db_ref[...] = finer(dot_nn, total, c_ref[...])
    dc_ref[...] = finer(dot_tn, total, b_ref[...])


def across_back_kernel(
    keep_ref, u_ref, dy_ref, dv_ref, ip_ref, halo_ref, local_ref, enter_ref, pref_ref, leave_ref,
    b_ref, c_ref, grow_ref, fall_ref, step_ref, skip_ref, dec_ref, taps_ref, spread_ref, select_ref,
    ig_ref, db_ref, q_ref, r_ref, end_ref, taps_grad_ref, bias_grad_ref, head_ref,
    state_ref, ext_ref, high_ref, low_ref, x_ref, fall_v_ref, state_low_ref, ends_ref,
):
    g = pl.program_id(0)
    c = pl.num_programs(0) - 1 - g
    width = u_ref.shape[1]
    keep = keep_ref[c].astype(F32)

    @pl.when(g == 0)
    def _():
        state_ref[...] = leave_ref[...].astype(F32)
        taps_grad_ref[...] = jnp.zeros_like(taps_grad_ref)
        bias_grad_ref[...] = jnp.zeros_like(bias_grad_ref)
        ext_ref[LEN : LEN + 8, :] = jnp.zeros((8, width), F32)

    @pl.when(g > 0)
    def _():
        ext_ref[LEN : LEN + 8, :] = ext_ref[0:8, :] * keep_ref[c + 1].astype(F32)

    b_map, b_low = halves(b_ref[...])
    c_map, c_low = halves(c_ref[...])
    grow = split_pair(grow_ref[...])
    fall = split_pair(fall_ref[...])
    steps = split_pair(step_ref[...])

    def step(i, carry):
        at = chunk(i, WIDE)
        spread = spread_ref[:, at]
        state = state_ref[:, at]
        state_low = state.astype(BF16)
        falling = dot_nn(fall, spread)
        across = falling * (dot_nn(b_map, state_low)+dot_nn(b_low, state_low))
        dv = dv_ref[:, at] + across
        u = u_ref[:, at]
        open_ = sigmoid(u)
        x = u * open_
        delta = dot_nn(steps, spread)
        v = x * delta
        v_low = v.astype(BF16).astype(F32)
        dy = dy_ref[:, at].astype(F32)
        dx = delta * dv + skip_ref[:, at] * dy
        ext_ref[0:LEN, at] = dx * (open_ * (1.0 + u * (1.0 - open_)))
        high_ref[:, at], low_ref[:, at] = halves(v_low * dv)
        x_ref[:, at] = (x * dv).astype(BF16)
        carried = (
            local_ref[0, :, at].astype(F32) + pref_ref[0, :, at] * enter_ref[:, at].astype(F32)
        ).astype(BF16)
        decay = dec_ref[0, :, at]
        end = jnp.sum(v_low * across, axis=0, keepdims=True) + decay * jnp.sum(
            state * carried.astype(F32), axis=0, keepdims=True
        )
        ends_ref[:, at] = jnp.broadcast_to(end, (8, WIDE))
        fall_v_ref[:, at] = (falling * v).astype(BF16)
        state_low_ref[:, at] = state_low
        z = (dot_nn(grow, spread) * dy).astype(BF16)
        state_ref[:, at] = keep * (decay * state + (dot_tn(c_map, z)+dot_tn(c_low,z)))
        return carry

    lax.fori_loop(0, width // WIDE, step, 0, unroll=2)
    select = select_ref[...]
    db_ref[...] = dot_nt(fall_v_ref[...], state_low_ref[...])
    q_ref[...] = dot_nn(high_ref[...], select) + dot_nn(low_ref[...], select)
    r_ref[...] = dot_nn(x_ref[...], select)
    end_ref[0] = head_sums(ends_ref[...], select)

    def conv(i, carry):
        at = chunk(i, WIDE)
        ip = ip_ref[:, at]
        du = ext_ref[0:LEN, at]
        bias_grad_ref[:, at] += jnp.sum(du, axis=0, keepdims=True)
        total = taps_ref[3:4, at] * du
        taps_grad_ref[3:4, at] += jnp.sum(ip * du, axis=0, keepdims=True)
        for lag in range(1, 4):
            later = ext_ref[lag : lag + LEN, at]
            total = total + taps_ref[3 - lag : 4 - lag, at] * later
            taps_grad_ref[3 - lag : 4 - lag, at] += jnp.sum(ip * later, axis=0, keepdims=True)
        ig_ref[:, at] = total.astype(BF16)
        return carry

    lax.fori_loop(0, width // WIDE, conv, 0, unroll=3)

    @pl.when(c == 0)
    def _():
        head_ref[...] = ext_ref[0:8, :] * keep
        for lag in range(1, 4):
            part = keep * ext_ref[0:lag, :] * halo_ref[HALO - lag : HALO, :]
            taps_grad_ref[3 - lag : 4 - lag, :] += jnp.sum(part, axis=0, keepdims=True)


def place_kernel(moves, count, outs, where_ref, *refs):
    pieces, out_refs = refs[:count], refs[count : count + outs]
    stages, casts, sems = refs[count + outs : 2 * count + outs], refs[2 * count + outs : -1], refs[-1]
    loads = []
    for i, piece in enumerate(pieces):
        load = pltpu.make_async_copy(piece, stages[i], sems.at[0, i])
        load.start()
        loads.append(load)
    stores, waited = [], set()
    for n, (i, t, window, out, row_slot, col_slot) in enumerate(moves):
        if i not in waited:
            loads[i].wait()
            waited.add(i)
        first, rows, left, width = window
        source = stages[i].at[t, pl.ds(first, rows), pl.ds(left, width)]
        if casts:
            cast = casts[n]
            cast[...] = source[...].astype(cast.dtype)
            source = cast
        row = pl.multiple_of(where_ref[row_slot], 16)
        if width == out_refs[out].shape[1]:
            target = out_refs[out].at[pl.ds(row, rows)]
        else:
            col = pl.multiple_of(where_ref[col_slot], 128)
            target = out_refs[out].at[pl.ds(row, rows), pl.ds(col, width)]
        store = pltpu.make_async_copy(source, target, sems.at[1, n])
        store.start()
        stores.append(store)
    for store in stores:
        store.wait()


def place(pieces, moves, shapes, dtype):
    slots, fixed = [], []
    for i, t, window, which, row, col in moves:
        window = window or (0, pieces[i].shape[1], 0, pieces[i].shape[2])
        fixed.append((i, t, window, which, len(slots), len(slots) + 1))
        slots += [jnp.asarray(row, jnp.int32), jnp.asarray(col, jnp.int32)]
    anywhere = pl.BlockSpec(memory_space=pl.ANY)
    casts = []
    if dtype != pieces[0].dtype:
        casts = [pltpu.VMEM((w[1], w[3]), dtype) for _, _, w, _, _, _ in fixed]
    nbytes = sum(2 * 2 * a * b for a, b in shapes)
    return pl.pallas_call(
        functools.partial(place_kernel, fixed, len(pieces), len(shapes)),
        in_specs=[pl.BlockSpec(memory_space=pltpu.SMEM)] + [anywhere] * len(pieces),
        out_specs=[anywhere] * len(shapes),
        out_shape=[jax.ShapeDtypeStruct(shape, dtype) for shape in shapes],
        scratch_shapes=[pltpu.VMEM(piece.shape, piece.dtype) for piece in pieces]
        + casts
        + [pltpu.SemaphoreType.DMA((2, max(len(pieces), len(moves))))],
        compiler_params=pltpu.CompilerParams(vmem_limit_bytes=VMEM),
        cost_estimate=pl.CostEstimate(flops=0, bytes_accessed=nbytes, transcendentals=0),
        name="place",
    )(jnp.stack(slots), *pieces)


def norm_kernel(pieces_ref, gain_ref, hid_ref, normed_ref):
    parts, rows, width = pieces_ref.shape
    squares = jnp.zeros((rows, 128), F32)
    for t in range(parts):
        v = pieces_ref[t].astype(F32)
        squares = squares + fold(v * v)
    mean = jnp.sum(squares, axis=1, keepdims=True) / (width * parts)
    factor = lax.rsqrt(mean + EPSILON)
    for t in range(parts):
        at = slice(t * width, (t + 1) * width)
        v = pieces_ref[t]
        hid_ref[:, at] = v
        normed_ref[:, at] = (v.astype(F32) * factor * gain_ref[:, at]).astype(BF16)


def join_kernel(pieces_ref, live_ref, out_ref):
    parts, _, width = pieces_ref.shape
    for t in range(parts):
        live = live_ref[...]
        out_ref[:, t * width : (t + 1) * width] = (pieces_ref[t].astype(F32) * live).astype(BF16)


def swap(v, mask, count):
    return lax.ppermute(v, "dp", [(i, i ^ mask) for i in range(count)])


def exchange(v):
    return lax.all_to_all(v, "tensor", 0, 0, tiled=True)


def rotate(v, by, count):
    return lax.ppermute(v, "tensor", [(i, (i + by) % count) for i in range(count)])


def in_order(pieces, column):
    return jnp.roll(jnp.stack([pieces[0]] + pieces[:0:-1]), column, axis=0)


def same_core(count):
    return [list(range(0, count, 2)), list(range(1, count, 2))]


def gather_chips(v, count):
    return [(v, 0)] + [(swap(v, mask, count), mask) for mask in range(2, count, 2)]


def gather_core(mine, count):
    return mine + [(swap(a, 1, count), mask ^ 1) for a, mask in mine]


def gather_pieces(v, count):
    return gather_core(gather_chips(v, count), count)


ANYWHERE = pl.BlockSpec(memory_space=pl.ANY)


def unread(count, extra):
    return lambda kernel: lambda *refs: kernel(*refs[:count], *refs[count + extra :])


def after(v, *first):
    first = jax.tree.leaves(first)
    return pl.pallas_call(
        lambda *refs: None,
        in_specs=[ANYWHERE] * (1 + len(first)),
        out_specs=ANYWHERE,
        out_shape=jax.ShapeDtypeStruct(v.shape, v.dtype),
        input_output_aliases={0: 0},
        cost_estimate=pl.CostEstimate(flops=0, bytes_accessed=0, transcendentals=0),
        name="after",
    )(v, *first)


def pair_lanes(v):
    wide = jnp.pad(v, ((0, 0), (0, 64 - v.shape[1])))
    return jnp.concatenate([wide, wide], axis=1)


def local(
    dp_count, tensor_count,
    hidden_in, out_grad, seq_lengths, seq_device, seq_offset, norm_gain, w_gate, w_input, w_shared,
    w_step, conv_inner, conv_shared, conv_inner_bias, conv_shared_bias, step_bias, decay_log,
    skip_gain, gate_norm_gain, w_output,
):
    parts = tensor_count
    dp = lax.axis_index("dp")
    column = lax.axis_index("tensor")
    core, q = dp & 1, dp >> 1
    rows_dev, piece = hidden_in.shape
    rows = rows_dev // parts
    blocks = rows // LEN
    model = norm_gain.shape[0]
    shard = w_input.shape[1]
    inner = shard * parts
    heads_shard = w_step.shape[1]
    heads = heads_shard * parts
    width = inner // heads
    nstate = w_shared.shape[1] // 2
    groups = dp_count // 2

    aligned = piece % 128 == 0
    turn = jnp.stack([(column - d) % parts for d in range(parts)]).astype(jnp.int32)

    def send_rows(v, halo):
        pieces = []
        for t in range(parts):
            pieces.append(v[t * rows : (t + 1) * rows])
            if halo:
                start = max(t * rows, HALO)
                pieces.append(v[start - HALO : start])
        size = rows + (HALO if halo else 0)
        return exchange(jnp.concatenate(pieces, axis=0).reshape(parts, size, piece))

    def send_back(v):
        pieces = [v[:, t * piece : (t + 1) * piece] for t in range(parts)]
        return jnp.stack(pieces)

    def row_block(size):
        return max(n for n in range(16, 129, 16) if size % n == 0)

    def join(kernel, pieces, extra, extra_rows, outs):
        size = pieces.shape[1]
        block = row_block(size)
        extra_spec = (
            pl.BlockSpec((block, 1), lambda g: (g, 0))
            if extra_rows
            else pl.BlockSpec(extra.shape, lambda g: (0, 0))
        )
        wide = pl.BlockSpec((block, model), lambda g: (g, 0))
        return pl.pallas_call(
            kernel,
            grid=(size // block,),
            in_specs=[pl.BlockSpec((parts, block, piece), lambda g: (0, g, 0)), extra_spec],
            out_specs=[wide] * outs,
            out_shape=[jax.ShapeDtypeStruct((size, model), BF16)] * outs,
            compiler_params=pltpu.CompilerParams(vmem_limit_bytes=VMEM),
            cost_estimate=pl.CostEstimate(
                flops=0, bytes_accessed=size * model * 2 * (1 + outs), transcendentals=0
            ),
            name="join",
        )(pieces, extra)

    def join_plain(pieces):
        return jnp.concatenate([pieces[t] for t in range(parts)], axis=1)

    k_rows = model // dp_count
    out_rows = shard // dp_count

    def slices_of(index):
        return index & 1, index >> 1

    def gather_all(v):
        return lax.all_gather(v, ("dp", "tensor"), axis=0)

    def my_rows(w, size):
        return lax.dynamic_slice_in_dim(w, dp * size, size, 0)

    def place_columns(slices):
        moves = [
            (0, j, None, 0, j // parts * k_rows, j % parts * shard) for j in range(slices.shape[0])
        ]
        return place([slices], moves, [(model, inner)], BF16)[0]

    def place_output(slices):
        moves = [
            (0, j, None, 0, j % parts * shard + j // parts * out_rows, 0)
            for j in range(slices.shape[0])
        ]
        return place([slices], moves, [(inner, model)], BF16)[0]

    place_dp = core * (model // 2) + q * k_rows

    vectors = jnp.concatenate([step_bias, decay_log, skip_gain])
    vectors = jnp.pad(vectors, (0, shard - vectors.shape[0]))[None, :]
    small = jnp.concatenate(
        [conv_inner, conv_inner_bias[None, :], gate_norm_gain[None, :], vectors], axis=0
    )
    terms = []
    for _ in range(3):
        term = lax.reduce_precision(small, 8, 7)
        terms.append(term.astype(BF16))
        small = small - term
    step_rows = model * heads_shard // shard
    small = jnp.concatenate(terms + [w_step.reshape(step_rows, shard)], axis=0)
    small_rows = -(-small.shape[0] // 16) * 16
    small = jnp.pad(small, ((0, small_rows - small.shape[0]), (0, 0)))
    first = lax.dynamic_slice_in_dim(w_input, place_dp, k_rows, 0)
    first = jnp.concatenate([first, small], axis=0)
    first = [first] + [rotate(first, d, parts) for d in range(1, parts)]
    hid_pieces = send_rows(hidden_in, True)
    small = in_order([v[k_rows:] for v in first], column)
    in_pieces = gather_pieces(jnp.stack([v[:k_rows] for v in first]), dp_count)
    terms = small[:, :21].astype(F32).reshape(parts, 3, 7, shard)
    terms = (terms[:, 0] + terms[:, 1]) + terms[:, 2]
    by_shard = lambda v: jnp.swapaxes(v, 0, 1).reshape(v.shape[1], inner)
    taps = by_shard(terms[:, :4])
    inner_bias = by_shard(terms[:, 4:5])
    gain_out = by_shard(terms[:, 5:6])
    by_head = lambda i: terms[:, 6, i * heads_shard : (i + 1) * heads_shard].reshape(1, heads)
    steps_bias = pair_lanes(by_head(0))
    logs = pair_lanes(by_head(1))
    skip_wide = jnp.repeat(by_head(2), width, axis=1)
    w_steps = small[:, 21 : 21 + step_rows].reshape(parts, model, heads_shard)
    w_steps = jnp.swapaxes(w_steps, 0, 1).reshape(model, heads)
    w_misc = jnp.concatenate([w_shared, pair_lanes(w_steps)], axis=1)
    misc_width = w_misc.shape[1]

    block_start = column * rows + jnp.arange(blocks + 1, dtype=jnp.int32) * LEN
    inside = (
        (seq_device[None, :] == dp)
        & (block_start[:, None] >= seq_offset[None, :])
        & (block_start[:, None] < seq_offset[None, :] + seq_lengths[None, :])
    )
    offset = jnp.sum(jnp.where(inside, block_start[:, None] - seq_offset[None, :], 0), axis=1)
    keep = (offset > 0).astype(jnp.int32)
    live_blocks = jnp.sum(inside.astype(F32), axis=1)[:blocks]
    live = jnp.repeat(live_blocks, LEN)[:, None]
    dev_start = jnp.arange(rows_dev // LEN, dtype=jnp.int32) * LEN
    dev_inside = (
        (seq_device[None, :] == dp)
        & (dev_start[:, None] >= seq_offset[None, :])
        & (dev_start[:, None] < seq_offset[None, :] + seq_lengths[None, :])
    )
    live_dev = jnp.repeat(jnp.sum(dev_inside.astype(F32), axis=1), LEN)[:, None]

    lane_head = jnp.arange(inner, dtype=jnp.int32) // width
    half_index = jnp.arange(128, dtype=jnp.int32) % 64
    spread = (half_index[:, None] == lane_head[None, :]).astype(BF16)
    select = (lane_head[:, None] == jnp.arange(128, dtype=jnp.int32)[None, :]).astype(BF16)
    columns = (
        (jnp.arange(192, dtype=jnp.int32) % 64)[:, None]
        == (jnp.arange(heads * LEN, dtype=jnp.int32) // LEN)[None, :]
    ).astype(BF16)

    if aligned:
        hid, normed_all = join(norm_kernel, hid_pieces, norm_gain[None, :], False, 2)
    else:
        hid = join_plain(hid_pieces)
        wide_in = hid.astype(F32)
        mean = jnp.mean(wide_in * wide_in, axis=1, keepdims=True)
        normed_all = (wide_in * lax.rsqrt(mean + EPSILON) * norm_gain[None, :]).astype(BF16)
    normed = normed_all[:rows]
    misc = dot_nn(normed_all, w_misc)

    params = pltpu.CompilerParams(vmem_limit_bytes=VMEM)
    smem = pl.BlockSpec(memory_space=pltpu.SMEM)
    full = lambda *shape: pl.BlockSpec(shape, lambda g: (0,) * len(shape))
    up = lambda *shape: pl.BlockSpec(shape, lambda g: (g,) + (0,) * (len(shape) - 1))
    down = lambda *shape: pl.BlockSpec(
        shape, lambda g: (blocks - 1 - g,) + (0,) * (len(shape) - 1)
    )
    out = jax.ShapeDtypeStruct
    cost = lambda flops, size: pl.CostEstimate(
        flops=flops, bytes_accessed=size, transcendentals=rows * inner
    )
    halo_block = lambda cols: pl.BlockSpec((HALO, cols), lambda g: (rows // HALO, 0))
    wide_map = 2 * rows * inner * nstate
    lanes = out((rows, 128), F32)

    (
        shared_u, b_map, c_map, delta2, slope2, rate2, cum3, cum_t, grow2, fall2, coef2, dec2,
    ) = pl.pallas_call(
        maps_kernel,
        grid=(blocks,),
        in_specs=[
            smem, up(LEN, misc_width), halo_block(misc_width), full(4, 2 * nstate),
            full(1, 2 * nstate), full(1, 128), full(1, 128),
        ],
        out_specs=[up(LEN, 2 * nstate)]
        + [up(LEN, 128)] * 5
        + [up(LEN, 192), pl.BlockSpec((128, LEN), lambda g: (0, g))]
        + [up(LEN, 128)] * 3
        + [up(1, 1, 128)],
        out_shape=[out((rows, 2 * nstate), F32)]
        + [lanes] * 5
        + [out((rows, 192), F32), out((128, rows), F32)]
        + [lanes] * 3
        + [out((blocks, 1, 128), F32)],
        scratch_shapes=[pltpu.VMEM((LEN + 8, 2 * nstate), F32)],
        compiler_params=params,
        cost_estimate=cost(0, rows * 128 * 4 * 16),
        name="maps",
    )(keep, misc, misc, conv_shared, conv_shared_bias[None, :], steps_bias, logs)

    moves = []
    for i, (_, mask) in enumerate(in_pieces):
        c2, q2 = slices_of(dp ^ mask)
        row = c2 * (model // 2) + q2 * k_rows
        moves += [(i, d, None, 0, row, turn[d] * shard) for d in range(parts)]
    moves.append((len(in_pieces), 0, None, 0, 0, inner))
    (w_in,) = place(
        [a for a, _ in in_pieces] + [w_misc[None]], moves, [(model, inner + misc_width)], BF16
    )
    gate_slices = gather_all(after(my_rows(w_gate, k_rows), *first[1:]))
    out_slices = None
    if out_rows % 16 == 0:
        out_slices = gather_all(after(my_rows(w_output, out_rows), *first[1:]))
    grad_pieces = send_rows(out_grad, False)
    inner_proj = dot_nn(normed_all, w_in[:, :inner])


    u, local_states, chunk_state, dec_wide, pref_wide, through = pl.pallas_call(
        conv_states_kernel,
        grid=(blocks,),
        in_specs=[
            smem, up(LEN, inner), halo_block(inner), full(4, inner), full(1, inner),
            up(LEN, nstate), up(LEN, 128), up(1, 1, 128), full(128, inner),
        ],
        out_specs=[
            up(LEN, inner), up(1, nstate, inner), full(nstate, inner), up(1, 1, inner),
            up(1, 1, inner), full(1, inner),
        ],
        out_shape=[
            out((rows, inner), F32), out((blocks, nstate, inner), BF16), out((nstate, inner), F32),
            out((blocks, 1, inner), F32), out((blocks, 1, inner), F32), out((1, inner), F32),
        ],
        scratch_shapes=[
            pltpu.VMEM((LEN + 8, inner), F32), pltpu.VMEM((nstate, inner), F32),
            pltpu.VMEM((1, inner), F32),
        ],
        compiler_params=params,
        cost_estimate=cost(2 * wide_map, rows * inner * 12),
        name="conv_states",
    )(keep, inner_proj, inner_proj, taps, inner_bias, b_map, coef2, dec2, spread)

    to_right = [(i, i + 1) for i in range(parts - 1)]
    to_left = [(i + 1, i) for i in range(parts - 1)]
    entering = lax.ppermute(chunk_state.astype(BF16), "tensor", to_right)

    heads_t = pl.BlockSpec((128, LEN), lambda g: (0, g))
    y_within = pl.pallas_call(
        within_kernel,
        grid=(blocks,),
        in_specs=[
            up(LEN, inner), up(LEN, 192), heads_t, up(LEN, 128), up(LEN, nstate),
            up(LEN, nstate), full(192, heads * LEN), full(128, inner),
        ],
        out_specs=up(LEN, inner),
        out_shape=out((rows, inner), F32),
        compiler_params=params,
        cost_estimate=cost(8 * wide_map, rows * inner * 8),
        name="within",
    )(
        u, cum3, cum_t, delta2, b_map, c_map, columns, spread
    )

    w_gates = place_columns(gate_slices)
    gate_proj = dot_nn(normed, w_gates)
    beside = [y_within, gate_proj]
    for i in range(parts - 2):
        entering = after(entering, *beside[i : i + 1])
        entering = lax.ppermute(
            (chunk_state + through * entering.astype(F32)).astype(BF16), "tensor", to_right
        )
    if out_slices is None:
        w_out = lax.all_gather(w_output, "tensor", axis=0, tiled=True)
    else:
        w_out = place_output(out_slices)

    if aligned:
        (masked,) = join(join_kernel, grad_pieces, live, True, 1)
    else:
        masked = join_plain(grad_pieces) * live.astype(BF16)
    normed_y_grad = dot_nt(masked, w_out)

    normed_y, scan_grad, gate_grad, q_plus, dc_across, gain_out_grad, skip_lanes, chunk_grad = (
        pl.pallas_call(
            gate_kernel,
            grid=(blocks,),
            in_specs=[
                smem, down(LEN, inner), down(LEN, inner), down(LEN, inner), down(LEN, inner),
                down(1, nstate, inner), full(nstate, inner), down(1, 1, inner), down(LEN, nstate),
                down(LEN, 128), full(1, inner), full(1, inner), down(1, 1, inner),
                full(128, inner), full(inner, 128),
            ],
            out_specs=[
                down(LEN, inner), down(LEN, inner), down(LEN, inner), down(LEN, 128),
                down(LEN, nstate), full(1, inner), full(1, inner), full(nstate, inner),
            ],
            out_shape=[
                out((rows, inner), BF16), out((rows, inner), BF16), out((rows, inner), BF16),
                lanes, out((rows, nstate), F32), out((1, inner), F32),
                out((1, inner), F32), out((nstate, inner), F32),
            ],
            scratch_shapes=[
                pltpu.VMEM((LEN, inner), F32), pltpu.VMEM((nstate, inner), BF16),
                pltpu.VMEM((nstate, inner), F32),
            ]
            + [pltpu.VMEM((LEN, inner), BF16)] * 3,
            compiler_params=params,
            cost_estimate=cost(6 * wide_map, rows * inner * 24),
            name="gate",
        )(
            keep, y_within, u, gate_proj, normed_y_grad, local_states, entering, pref_wide, c_map,
            grow2, skip_wide, gain_out, dec_wide, spread, select,
        )
    )

    leaving = lax.ppermute(chunk_grad.astype(BF16), "tensor", to_left)

    def half_of(v, which):
        size = v.shape[1] // 2
        return lax.dynamic_slice_in_dim(v, which * size, size, 1)

    out_sent = swap(dot_tn(normed_y, half_of(masked, 1 - core)).astype(BF16), 1, dp_count)
    gate_sent = swap(dot_tn(half_of(normed, 1 - core), gate_grad).astype(BF16), 1, dp_count)
    gate_part = dot_nt(gate_grad, w_gates)
    mixed_rows = dot_nn(normed_y, w_out).astype(BF16)
    out_total = (dot_tn(normed_y, half_of(masked, core)) + out_sent.astype(F32)).astype(BF16)
    beside = [[gate_part], [out_total, mixed_rows]]
    for i in range(parts - 2):
        leaving = after(leaving, *(beside[i] if i < len(beside) else []))
        if i == 1:
            mixed_sent = after(send_back(mixed_rows), leaving)
        leaving = lax.ppermute(
            (chunk_grad + through * leaving.astype(F32)).astype(BF16), "tensor", to_left
        )
    gate_total = (dot_tn(half_of(normed, core), gate_grad) + gate_sent.astype(F32)).astype(BF16)
    out_group = shard // groups
    group_rows = model // dp_count
    half_model = model // 2

    def chip_sum(v):
        return lax.psum_scatter(
            v, "dp", scatter_dimension=0, axis_index_groups=same_core(dp_count), tiled=False
        )

    def shard_sum(v):
        mine = lax.psum_scatter(v, "tensor", scatter_dimension=0, tiled=False)
        return lax.all_gather(mine, "dp", axis=0)

    out_sum = chip_sum(
        jnp.swapaxes(out_total.reshape(parts, groups, out_group, half_model), 0, 1)
    )
    gate_sum = chip_sum(gate_total.reshape(groups, group_rows, inner))
    out_parts = shard_sum(out_sum)
    gate_parts = shard_sum(
        jnp.stack([gate_sum[:, t * shard : (t + 1) * shard] for t in range(parts)])
    )

    dv_within, db_within, dc_within = pl.pallas_call(
        unread(9, 1)(within_back_kernel),
        grid=(blocks,),
        in_specs=[
            up(LEN, inner), up(LEN, inner), up(LEN, 192), heads_t, up(LEN, 128), up(LEN, nstate),
            up(LEN, nstate), full(192, heads * LEN), full(128, inner), ANYWHERE,
        ],
        out_specs=[up(LEN, inner), up(LEN, nstate), up(LEN, nstate)],
        out_shape=[out((rows, inner), F32), out((rows, nstate), F32), out((rows, nstate), F32)],
        compiler_params=params,
        cost_estimate=cost(16 * wide_map, rows * inner * 10),
        name="within_back",
    )(u, scan_grad, cum3, cum_t, delta2, b_map, c_map, columns, spread, gate_part)


    grads, db_across, q_minus, step_sums, end_sums, taps_grad, bias_grad, head_rows = (
        pl.pallas_call(
            across_back_kernel,
            grid=(blocks,),
            in_specs=[
                smem, down(LEN, inner), down(LEN, inner), down(LEN, inner), down(LEN, inner),
                halo_block(inner), down(1, nstate, inner), full(nstate, inner), down(1, 1, inner),
                full(nstate, inner), down(LEN, nstate), down(LEN, nstate), down(LEN, 128),
                down(LEN, 128), down(LEN, 128), full(1, inner), down(1, 1, inner), full(4, inner),
                full(128, inner), full(inner, 128),
            ],
            out_specs=[
                down(LEN, inner), down(LEN, nstate), down(LEN, 128), down(LEN, 128),
                down(1, 8, 128), full(4, inner), full(1, inner), full(8, inner),
            ],
            out_shape=[
                out((rows, inner + misc_width), BF16), out((rows, nstate), F32), lanes, lanes,
                out((blocks, 8, 128), F32), out((4, inner), F32), out((1, inner), F32),
                out((8, inner), F32),
            ],
            scratch_shapes=[
                pltpu.VMEM((nstate, inner), F32), pltpu.VMEM((LEN + 8, inner), F32),
            ]
            + [pltpu.VMEM((LEN, inner), BF16)] * 5
            + [pltpu.VMEM((8, inner), F32)],
            compiler_params=params,
            cost_estimate=cost(6 * wide_map, rows * inner * 20),
            name="across_back",
        )(
            keep, u, scan_grad, dv_within, inner_proj, inner_proj, local_states,
            entering, pref_wide, after(leaving, dv_within, gate_total), b_map, c_map, grow2, fall2, delta2, skip_wide, dec_wide, taps,
            spread, select,
        )
    )

    misc_at = inner // misc_width
    mixer_part = exchange(mixed_sent)
    grads, shared_taps_grad, shared_bias_grad, shared_head, vectors = pl.pallas_call(
        unread(17, 1)(maps_back_kernel),
        grid=(blocks,),
        in_specs=[
            smem, down(LEN, nstate), down(LEN, nstate), down(LEN, nstate), down(LEN, nstate),
            down(LEN, 2 * nstate), down(LEN, misc_width), halo_block(misc_width),
            full(4, 2 * nstate), down(LEN, 128), down(LEN, 128), down(LEN, 128), down(1, 8, 128),
            down(LEN, 128), down(LEN, 128), full(1, 128), ANYWHERE, ANYWHERE,
        ],
        out_specs=[
            pl.BlockSpec((LEN, misc_width), lambda g: (blocks - 1 - g, misc_at)),
            full(4, 2 * nstate), full(1, 2 * nstate), full(8, 2 * nstate), full(8, 128),
        ],
        out_shape=[
            out((rows, inner + misc_width), BF16), out((4, 2 * nstate), F32),
            out((1, 2 * nstate), F32), out((8, 2 * nstate), F32), out((8, 128), F32),
        ],
        input_output_aliases={16: 0},
        scratch_shapes=[pltpu.VMEM((LEN + 8, 2 * nstate), F32)],
        compiler_params=params,
        cost_estimate=cost(0, rows * 128 * 4 * 16),
        name="maps_back",
    )(
        keep, db_within, db_across, dc_within, dc_across, shared_u, misc, misc, conv_shared,
        q_plus, q_minus, step_sums, end_sums, slope2, rate2, logs, grads, mixer_part,
    )
    mixer_part = mixer_part.reshape(rows_dev, piece).astype(F32)
    mixed_out = (hidden_in.astype(F32) + live_dev * mixer_part).astype(BF16)

    next_heads = lax.ppermute(
        jnp.concatenate([head_rows, shared_head], axis=1), "tensor", to_left
    )
    all_taps = jnp.concatenate([taps, conv_shared], axis=1)
    reach = inner + 2 * nstate
    last_rows = lax.dynamic_slice(grads, (rows - 16, 0), (16, reach)).astype(F32)
    for lag in range(1, 4):
        moved = jnp.pad(next_heads[:lag], ((16 - lag, 0), (0, 0)))
        last_rows = last_rows + all_taps[3 - lag][None, :] * moved
    grads = lax.dynamic_update_slice(grads, last_rows.astype(BF16), (rows - 16, 0))

    in_sent = swap(dot_tn(half_of(normed, 1 - core), grads).astype(BF16), 1, dp_count)
    normed_grad = gate_part + dot_nt(grads, w_in)
    input_grad, norm_gain_grad = pl.pallas_call(
        input_grad_kernel,
        grid=(blocks,),
        in_specs=[up(LEN, model), up(LEN, model), full(1, model)],
        out_specs=[up(LEN, model), full(1, model)],
        out_shape=[out((rows, model), BF16), out((1, model), F32)],
        compiler_params=params,
        cost_estimate=cost(0, rows * model * 8),
        name="input_grad",
    )(normed_grad, hid, norm_gain[None, :])

    tiny = jnp.concatenate(
        [
            shared_taps_grad.reshape(1, -1), shared_bias_grad, vectors[0:1], vectors[1:2],
            norm_gain_grad,
        ],
        axis=1,
    )
    tiny = jnp.pad(tiny, ((0, 0), (0, inner - tiny.shape[1])))
    tiny = jnp.concatenate([taps_grad, bias_grad, gain_out_grad, skip_lanes, tiny], axis=0)
    tiny = tiny + swap(tiny, 1, dp_count)

    def two_terms(v):
        high = lax.reduce_precision(v, 8, 7)
        return jnp.concatenate([high, v - high], axis=0).astype(BF16)

    def one_term(v):
        return v[:8].astype(F32) + v[8:].astype(F32)

    in_total = (dot_tn(half_of(normed, core), grads) + in_sent.astype(F32)).astype(BF16)
    tiny_low = jnp.pad(two_terms(tiny), ((0, 0), (0, misc_width)))
    in_part = lambda which: jnp.concatenate(
        [lax.dynamic_slice_in_dim(in_total, which * k_rows, k_rows, 0), tiny_low], axis=0
    )
    in_received = [in_part(q)]
    for mask in range(1, groups):
        in_received.append(swap(in_part(q ^ mask), 2 * mask, dp_count))
    tiny = [one_term(v[k_rows:, :inner]) for v in in_received]
    while len(tiny) > 1:
        tiny = [tiny[i] + tiny[i + 1] for i in range(0, len(tiny), 2)]
    tiny_low = two_terms(tiny[0])
    in_group = in_received[0][:k_rows].astype(F32)
    for v in in_received[1:]:
        in_group = in_group + v[:k_rows].astype(F32)
    in_group = in_group.astype(BF16)
    cols = shard + misc_width
    lengths = -(-inner // cols)
    tiny_low = jnp.pad(tiny_low, ((0, 0), (0, lengths * cols - inner)))
    tiny_low = jnp.concatenate([tiny_low[:, i * cols : (i + 1) * cols] for i in range(lengths)])
    in_sends = []
    for t in range(parts):
        mine = [in_group[:, t * shard : (t + 1) * shard], in_group[:, inner:]]
        in_sends.append(jnp.concatenate([jnp.concatenate(mine, axis=1), tiny_low], axis=0))
    hidden_sent = send_back(input_grad)
    hidden_part = exchange(hidden_sent)
    in_arrived = exchange(jnp.stack(in_sends))
    in_shard = jnp.sum(in_arrived[:, :k_rows].astype(F32), axis=0).astype(BF16)
    tiny_low = in_arrived[:, k_rows:].reshape(parts, lengths, 2, 8, cols).astype(F32)
    tiny = jnp.sum(tiny_low[:, :, 0] + tiny_low[:, :, 1], axis=0)
    tiny = jnp.concatenate([tiny[i] for i in range(lengths)], axis=1)
    own_columns = lax.dynamic_slice_in_dim(tiny[:7], column * shard, shard, 1)
    ends_at = [0]
    for size in (8 * nstate, 2 * nstate, 128, 128, model):
        ends_at.append(ends_at[-1] + size)
    part = lambda i: tiny[7, ends_at[i] : ends_at[i + 1]]
    own_heads = lambda v: lax.dynamic_slice_in_dim(v, column * heads_shard, heads_shard, 0)

    w_output_grad = (
        out_parts.reshape(groups, 2, out_group, half_model)
        .transpose(0, 2, 1, 3)
        .reshape(shard, model)
        .astype(F32)
    )
    w_gate_grad = (
        gate_parts.reshape(groups, 2, group_rows, shard)
        .transpose(1, 0, 2, 3)
        .reshape(model, shard)
        .astype(F32)
    )
    in_pieces = gather_pieces(in_shard[None], dp_count)
    moves = []
    for i, (_, mask) in enumerate(in_pieces):
        c2, q2 = slices_of(dp ^ mask)
        row = c2 * half_model + q2 * k_rows
        moves.append((i, 0, (0, k_rows, 0, shard), 0, row, 0))
        moves.append((i, 0, (0, k_rows, shard, 2 * nstate), 1, row, 0))
        moves.append((i, 0, (0, k_rows, shard + 2 * nstate, 128), 2, row, 0))
    w_input_grad, w_shared_grad, step_lanes = place(
        [a for a, _ in in_pieces],
        moves,
        [(model, shard), (model, 2 * nstate), (model, 128)],
        F32,
    )
    w_step_grad = lax.dynamic_slice_in_dim(step_lanes, column * heads_shard, heads_shard, 1)
    hidden_grad = hidden_part.reshape(rows_dev, piece).astype(F32) + out_grad.astype(F32)

    return (
        mixed_out,
        hidden_grad,
        part(4),
        w_gate_grad,
        w_input_grad,
        w_shared_grad,
        w_step_grad,
        own_columns[:4],
        part(0).reshape(4, 2 * nstate),
        own_columns[4],
        part(1),
        own_heads(part(2)),
        own_heads(part(3)),
        jnp.sum(own_columns[6].reshape(heads_shard, width), axis=1),
        own_columns[5],
        w_output_grad,
    )


def solution(mesh):
    split = P("tensor")
    in_specs = (
        P("dp", "tensor"), P("dp", "tensor"), P(), P(), P(), P(), P(None, "tensor"),
        P(None, "tensor"), P(), P(None, "tensor"), P(None, "tensor"), P(), split, P(), split,
        split, split, split, P("tensor", None),
    )
    out_specs = (
        P("dp", "tensor"), P("dp", "tensor"), P(), P(None, "tensor"), P(None, "tensor"), P(),
        P(None, "tensor"), P(None, "tensor"), P(), split, P(), split, split, split, split,
        P("tensor", None),
    )
    body = functools.partial(local, mesh.shape["dp"], mesh.shape["tensor"])
    return jax.shard_map(body, mesh=mesh, in_specs=in_specs, out_specs=out_specs, check_vma=False)
```

```python
import functools

import jax
import jax.numpy as jnp
from jax import lax
from jax.experimental import pallas as pl
from jax.experimental.pallas import tpu as pltpu
from jax.sharding import PartitionSpec as P

F32 = jnp.float32
BF16 = jnp.bfloat16
PRECISE = lax.Precision.HIGHEST
EPSILON = 1e-05
LEN = 128
HALO = 16
WIDE = 256
VMEM = 52 * 1024 * 1024


def dot_nn(a, b):
    return jnp.dot(a, b, preferred_element_type=F32)


def dot_nt(a, b):
    return lax.dot_general(a, b, (((1,), (1,)), ((), ())), preferred_element_type=F32)


def dot_tn(a, b):
    return lax.dot_general(a, b, (((0,), (0,)), ((), ())), preferred_element_type=F32)


def sigmoid(v):
    return 0.5 * jnp.tanh(0.5 * v) + 0.5


def split_pair(v):
    lane = lax.broadcasted_iota(jnp.int32, v.shape, 1)
    high = v.astype(BF16).astype(F32)
    return jnp.where(lane < 64, high, v - high).astype(BF16)


def split_triple(v):
    lane = lax.broadcasted_iota(jnp.int32, v.shape, 1)
    high = v.astype(BF16).astype(F32)
    rest = v - high
    middle = rest.astype(BF16).astype(F32)
    return jnp.where(lane < 64, high, jnp.where(lane < 128, middle, rest - middle)).astype(BF16)


def head_sums(v, select):
    high = v.astype(BF16)
    low = (v - high.astype(F32)).astype(BF16)
    return dot_nn(high, select) + dot_nn(low, select)


def halves(v):
    high = v.astype(BF16)
    return high, (v - high.astype(F32)).astype(BF16)


def finer(dot, a, b):
    a_high, a_low = halves(a)
    b_high, b_low = halves(b)
    return dot(a_high, b_high) + (dot(a_high, b_low) + dot(a_low, b_high))


def fold(v):
    total = v[:, :128]
    for i in range(1, v.shape[1] // 128):
        total = total + v[:, i * 128 : (i + 1) * 128]
    return total


def two_heads(first, v):
    v = v.astype(F32)
    return jnp.concatenate(
        [jnp.where(first, v, 0.0).astype(BF16), jnp.where(first, 0.0, v).astype(BF16)], axis=0
    )


def chunk(i, width):
    return pl.ds(pl.multiple_of(i * width, width), width)


def maps_kernel(
    keep_ref, misc_ref, halo_ref, taps_ref, bias_ref, step_bias_ref, logs_ref,
    u_ref, b_ref, c_ref, step_ref, slope_ref, rate_ref, cum_ref, cum_t_ref, grow_ref, fall_ref,
    coef_ref, dec_ref, ext_ref,
):
    c = pl.program_id(0)
    keep = keep_ref[c].astype(F32)
    shared = u_ref.shape[1]

    @pl.when(c == 0)
    def _():
        ext_ref[0:8, :] = halo_ref[8:16, :shared] * keep

    @pl.when(c > 0)
    def _():
        ext_ref[0:8, :] = ext_ref[LEN : LEN + 8, :] * keep

    ext_ref[8 : LEN + 8, :] = misc_ref[:, :shared]
    u = bias_ref[...] + taps_ref[3:4, :] * ext_ref[8 : 8 + LEN, :]
    for lag in range(1, 4):
        u = u + taps_ref[3 - lag : 4 - lag, :] * ext_ref[8 - lag : 8 - lag + LEN, :]
    u_ref[...] = u
    maps = u * sigmoid(u)
    b_ref[...] = maps[:, : shared // 2]
    c_ref[...] = maps[:, shared // 2 :]

    raw = misc_ref[:, shared:] + step_bias_ref[...]
    step = jnp.maximum(raw, 0.0) + jnp.log1p(jnp.exp(-jnp.abs(raw)))
    slope_ref[...] = sigmoid(raw)
    step_ref[...] = step
    rates = -step * jnp.exp(logs_ref[...])
    rate_ref[...] = rates
    cum = running_sum(rates, False)
    cum_ref[...] = jnp.concatenate([cum, cum[:, :64]], axis=1)
    cum_t_ref[...] = cum.T
    last = cum[LEN - 1 : LEN, :]
    fall = jnp.exp(last - cum)
    grow_ref[...] = jnp.exp(cum)
    fall_ref[...] = fall
    coef_ref[...] = fall * step
    dec_ref[0] = jnp.exp(last)


def running_sum(v, backwards):
    row = lax.broadcasted_iota(jnp.int32, (LEN, LEN), 0)
    col = lax.broadcasted_iota(jnp.int32, (LEN, LEN), 1)
    ones = jnp.where((row <= col) if backwards else (row >= col), 1.0, 0.0).astype(BF16)
    total = jnp.zeros(v.shape, F32)
    for _ in range(3):
        term = v.astype(BF16)
        total = total + dot_nn(ones, term)
        v = v - term.astype(F32)
    return total


def maps_back_kernel(
    keep_ref, db1_ref, db2_ref, dc1_ref, dc2_ref, u_ref, misc_ref, halo_ref, taps_ref, plus_ref,
    minus_ref, sums_ref, ends_ref, slope_ref, rate_ref, logs_ref, whole_ref,
    grad_ref, taps_grad_ref, bias_grad_ref, head_ref, vector_ref, ext_ref,
):
    g = pl.program_id(0)
    c = pl.num_programs(0) - 1 - g
    keep = keep_ref[c].astype(F32)
    shared = u_ref.shape[1]

    @pl.when(g == 0)
    def _():
        taps_grad_ref[...] = jnp.zeros_like(taps_grad_ref)
        bias_grad_ref[...] = jnp.zeros_like(bias_grad_ref)
        vector_ref[...] = jnp.zeros_like(vector_ref)
        ext_ref[LEN : LEN + 8, :] = jnp.zeros((8, shared), F32)

    @pl.when(g > 0)
    def _():
        ext_ref[LEN : LEN + 8, :] = ext_ref[0:8, :] * keep_ref[c + 1].astype(F32)

    u = u_ref[...]
    open_ = sigmoid(u)
    dmaps = jnp.concatenate([db1_ref[...] + db2_ref[...], dc1_ref[...] + dc2_ref[...]], axis=1)
    du = dmaps * (open_ * (1.0 + u * (1.0 - open_)))
    ext_ref[0:LEN, :] = du
    proj = misc_ref[:, :shared]
    bias_grad_ref[...] += jnp.sum(du, axis=0, keepdims=True)
    total = taps_ref[3:4, :] * du
    taps_grad_ref[3:4, :] += jnp.sum(proj * du, axis=0, keepdims=True)
    for lag in range(1, 4):
        later = ext_ref[lag : lag + LEN, :]
        total = total + taps_ref[3 - lag : 4 - lag, :] * later
        taps_grad_ref[3 - lag : 4 - lag, :] += jnp.sum(proj * later, axis=0, keepdims=True)
    da = running_sum(plus_ref[...] - minus_ref[...], True) + ends_ref[0, 0:1, :]
    raw_grad = (sums_ref[...] - da * jnp.exp(logs_ref[...])) * slope_ref[...]
    grad_ref[...] = jnp.concatenate([total, raw_grad], axis=1).astype(BF16)
    vector_ref[0:1, :] += jnp.sum(raw_grad, axis=0, keepdims=True)
    vector_ref[1:2, :] += jnp.sum(da * rate_ref[...], axis=0, keepdims=True)

    @pl.when(c == 0)
    def _():
        head_ref[...] = ext_ref[0:8, :] * keep
        for lag in range(1, 4):
            part = keep * ext_ref[0:lag, :] * halo_ref[HALO - lag : HALO, :shared]
            taps_grad_ref[3 - lag : 4 - lag, :] += jnp.sum(part, axis=0, keepdims=True)


def input_grad_kernel(ng_ref, hid_ref, gain_ref, out_ref, gain_grad_ref):
    @pl.when(pl.program_id(0) == 0)
    def _():
        gain_grad_ref[...] = jnp.zeros_like(gain_grad_ref)

    width = ng_ref.shape[1]
    u = hid_ref[...].astype(F32)
    ng = ng_ref[...]
    factor = lax.rsqrt(jnp.sum(fold(u * u), axis=1, keepdims=True) / width + EPSILON)
    gain_grad_ref[...] += jnp.sum(ng * u * factor, axis=0, keepdims=True)
    weighted = ng * gain_ref[...]
    stat = jnp.sum(fold(weighted * u), axis=1, keepdims=True) / width
    out_ref[...] = (factor * weighted - u * (factor * factor * factor * stat)).astype(BF16)


def conv_states_kernel(
    keep_ref, ip_ref, halo_ref, taps_ref, bias_ref, b_ref, coef_ref, dec_ref, spread_ref,
    u_ref, local_ref, out_ref, wide_ref, pref_ref, through_ref, ext_ref, state_ref, run_ref,
):
    c = pl.program_id(0)
    keep = keep_ref[c].astype(F32)

    @pl.when(c == 0)
    def _():
        state_ref[...] = jnp.zeros_like(state_ref)
        run_ref[...] = jnp.ones_like(run_ref)
        ext_ref[0:8, :] = halo_ref[8:16, :] * keep

    @pl.when(c > 0)
    def _():
        ext_ref[0:8, :] = ext_ref[LEN : LEN + 8, :] * keep

    ext_ref[8 : LEN + 8, :] = ip_ref[...]
    coef = split_pair(coef_ref[...])
    dec = split_pair(jnp.broadcast_to(dec_ref[0], (8, 128)))
    b_map, b_low = halves(b_ref[...])

    def step(i, carry):
        at = chunk(i, WIDE)
        u = bias_ref[:, at] + taps_ref[3:4, at] * ext_ref[8 : 8 + LEN, at]
        for lag in range(1, 4):
            u = u + taps_ref[3 - lag : 4 - lag, at] * ext_ref[8 - lag : 8 - lag + LEN, at]
        u_ref[:, at] = u
        spread = spread_ref[:, at]
        w = (u * sigmoid(u) * dot_nn(coef, spread)).astype(BF16)
        state = state_ref[:, at] * keep
        local_ref[0, :, at] = state
        decay = dot_nn(dec, spread)[0:1, :]
        wide_ref[0, :, at] = decay
        pref = run_ref[:, at] * keep
        pref_ref[0, :, at] = pref
        run_ref[:, at] = pref * decay
        state_ref[:, at] = decay * state + (dot_tn(b_map, w) + dot_tn(b_low, w))
        return carry

    lax.fori_loop(0, u_ref.shape[1] // WIDE, step, 0, unroll=3)

    @pl.when(c == pl.num_programs(0) - 1)
    def _():
        out_ref[...] = state_ref[...]
        through_ref[...] = run_ref[...]


def within_kernel(
    u_ref, cum_ref, cum_t_ref, step_ref, b_ref, c_ref, columns_ref, spread_ref, y_ref
):
    scores = finer(dot_nt, c_ref[...], b_ref[...])
    row = lax.broadcasted_iota(jnp.int32, (LEN, LEN), 0)
    col = lax.broadcasted_iota(jnp.int32, (LEN, LEN), 1)
    scores = jnp.where(row >= col, scores, 0.0)
    scores = jnp.concatenate([scores, scores], axis=1)
    cum = split_triple(cum_ref[...])
    steps = split_pair(step_ref[...])
    first = col < 64

    def pair(p, carry):
        at = chunk(p, 128)
        left = dot_nn(cum, columns_ref[:, chunk(p, 256)])
        right = jnp.concatenate(
            [cum_t_ref[pl.ds(2 * p, 1), :], cum_t_ref[pl.ds(2 * p + 1, 1), :]], axis=1
        )
        mixing = (jnp.exp(jnp.minimum(left - right, 0.0)) * scores).astype(BF16)
        u = u_ref[:, at]
        v = u * sigmoid(u) * dot_nn(steps, spread_ref[:, at])
        v, v_rest = halves(v)
        y_ref[:, at] = dot_nn(mixing, two_heads(first, v)) + dot_nn(
            mixing, two_heads(first, v_rest)
        )
        return carry

    lax.fori_loop(0, u_ref.shape[1] // 128, pair, 0, unroll=8)


def gate_kernel(
    keep_ref, y_ref, u_ref, gate_ref, ng_ref, local_ref, enter_ref, pref_ref, c_ref, grow_ref,
    skip_ref, gain_ref, dec_ref, spread_ref, select_ref,
    ny_ref, dy_ref, gg_ref, q_ref, dc_ref, gain_grad_ref, skip_grad_ref, out_ref,
    scan_ref, carried_ref, state_ref, high_ref, low_ref, z_ref, rest_ref, z_low_ref,
):
    g = pl.program_id(0)
    c = pl.num_programs(0) - 1 - g
    width = y_ref.shape[1]
    keep = keep_ref[c].astype(F32)

    @pl.when(g == 0)
    def _():
        state_ref[...] = jnp.zeros_like(state_ref)
        gain_grad_ref[...] = jnp.zeros_like(gain_grad_ref)
        skip_grad_ref[...] = jnp.zeros_like(skip_grad_ref)

    c_map, c_low = halves(c_ref[...])
    grow = split_pair(grow_ref[...])

    def forward(i, sums):
        squares, stat = sums
        at = chunk(i, WIDE)
        carried, rest = halves(
            local_ref[0, :, at] + pref_ref[0, :, at] * enter_ref[:, at].astype(F32)
        )
        carried_ref[:, at] = carried
        rest_ref[:, at] = rest
        scanned = y_ref[:, at] + dot_nn(grow, spread_ref[:, at]) * (
            dot_nn(c_map, carried) + (dot_nn(c_low, carried) + dot_nn(c_map, rest))
        )
        scan_ref[:, at] = scanned
        u = u_ref[:, at]
        y = scanned + skip_ref[:, at] * (u * sigmoid(u))
        gate = gate_ref[:, at]
        gated = y * (gate * sigmoid(gate))
        squares = squares + fold(gated * gated)
        stat = stat + fold(ng_ref[:, at] * gain_ref[:, at] * gated)
        return (squares, stat)

    nothing = jnp.zeros((LEN, 128), F32)
    squares, stat = lax.fori_loop(0, width // WIDE, forward, (nothing, nothing), unroll=3)
    scale = lax.rsqrt(jnp.sum(squares, axis=1, keepdims=True) / width + EPSILON)
    back = scale * scale * scale * (jnp.sum(stat, axis=1, keepdims=True) / width)

    def backward(i, carry):
        at = chunk(i, WIDE)
        scanned = scan_ref[:, at]
        u = u_ref[:, at]
        x = u * sigmoid(u)
        y = scanned + skip_ref[:, at] * x
        gate = gate_ref[:, at]
        open_ = sigmoid(gate)
        act = gate * open_
        gated = y * act
        scaled = gated * scale
        ng = ng_ref[:, at]
        gain = gain_ref[:, at]
        ny_ref[:, at] = (scaled * gain).astype(BF16)
        gain_grad_ref[:, at] += jnp.sum(ng * scaled, axis=0, keepdims=True)
        gated_grad = scale * (ng * gain) - gated * back
        gg_ref[:, at] = (gated_grad * y * open_ * (1.0 + gate * (1.0 - open_))).astype(BF16)
        dy = gated_grad * act
        dy_ref[:, at] = dy
        skip_grad_ref[:, at] += jnp.sum(dy * x, axis=0, keepdims=True)
        high_ref[:, at], low_ref[:, at] = halves(dy * scanned)
        z, z_low = halves(dot_nn(grow, spread_ref[:, at]) * dy)
        z_ref[:, at] = z
        z_low_ref[:, at] = z_low
        state_ref[:, at] = keep * (dec_ref[0, :, at] * state_ref[:, at] + (dot_tn(c_map, z) + (dot_tn(c_low, z) + dot_tn(c_map, z_low))))
        return carry

    lax.fori_loop(0, width // WIDE, backward, 0, unroll=3)
    select = select_ref[...]
    q_ref[...] = dot_nn(high_ref[...], select) + dot_nn(low_ref[...], select)
    z = z_ref[...]
    carried = carried_ref[...]
    dc_ref[...] = dot_nt(z, carried) + (dot_nt(z, rest_ref[...]) + dot_nt(z_low_ref[...], carried))

    @pl.when(c == 0)
    def _():
        out_ref[...] = state_ref[...]


def within_back_kernel(
    u_ref, dy_ref, cum_ref, cum_t_ref, step_ref, b_ref, c_ref, columns_ref, spread_ref,
    dv_ref, db_ref, dc_ref,
):
    scores = finer(dot_nt, b_ref[...], c_ref[...])
    row = lax.broadcasted_iota(jnp.int32, (LEN, LEN), 0)
    col = lax.broadcasted_iota(jnp.int32, (LEN, LEN), 1)
    scores = jnp.where(row <= col, scores, 0.0)
    scores = jnp.concatenate([scores, scores], axis=1)
    cum = split_triple(cum_ref[...])
    steps = split_pair(step_ref[...])
    first = col < 64

    def pair(p, total):
        at = chunk(p, 128)
        left = dot_nn(cum, columns_ref[:, chunk(p, 256)])
        right = jnp.concatenate(
            [cum_t_ref[pl.ds(2 * p, 1), :], cum_t_ref[pl.ds(2 * p + 1, 1), :]], axis=1
        )
        decay = jnp.exp(jnp.minimum(right - left, 0.0))
        mixing = (decay * scores).astype(BF16)
        dy, dy_rest = halves(dy_ref[:, at])
        dv_ref[:, at] = dot_nn(mixing, two_heads(first, dy)) + dot_nn(
            mixing, two_heads(first, dy_rest)
        )
        u = u_ref[:, at]
        v = u * sigmoid(u) * dot_nn(steps, spread_ref[:, at])
        v_stack = two_heads(first, v)
        dw = dot_nt(v_stack, dy) + dot_nt(v_stack, dy_rest)
        return total + decay[:, :LEN] * dw[:LEN] + decay[:, LEN:] * dw[LEN:]

    total = lax.fori_loop(
        0, u_ref.shape[1] // 128, pair, jnp.zeros((LEN, LEN), F32), unroll=8
    )
    total = jnp.where(row <= col, total, 0.0)
    db_ref[...] = finer(dot_nn, total, c_ref[...])
    dc_ref[...] = finer(dot_tn, total, b_ref[...])


def across_back_kernel(
    keep_ref, u_ref, dy_ref, dv_ref, ip_ref, halo_ref, local_ref, enter_ref, pref_ref, leave_ref,
    b_ref, c_ref, grow_ref, fall_ref, step_ref, skip_ref, dec_ref, taps_ref, spread_ref, select_ref,
    ig_ref, db_ref, q_ref, r_ref, end_ref, taps_grad_ref, bias_grad_ref, head_ref,
    state_ref, ext_ref, high_ref, low_ref, x_ref, fall_v_ref, state_low_ref, rest_ref, fall_rest_ref, ends_ref,
):
    g = pl.program_id(0)
    c = pl.num_programs(0) - 1 - g
    width = u_ref.shape[1]
    keep = keep_ref[c].astype(F32)

    @pl.when(g == 0)
    def _():
        state_ref[...] = leave_ref[...].astype(F32)
        taps_grad_ref[...] = jnp.zeros_like(taps_grad_ref)
        bias_grad_ref[...] = jnp.zeros_like(bias_grad_ref)
        ext_ref[LEN : LEN + 8, :] = jnp.zeros((8, width), F32)

    @pl.when(g > 0)
    def _():
        ext_ref[LEN : LEN + 8, :] = ext_ref[0:8, :] * keep_ref[c + 1].astype(F32)

    b_map, b_low = halves(b_ref[...])
    c_map, c_low = halves(c_ref[...])
    grow = split_pair(grow_ref[...])
    fall = split_pair(fall_ref[...])
    steps = split_pair(step_ref[...])

    def step(i, carry):
        at = chunk(i, WIDE)
        spread = spread_ref[:, at]
        state = state_ref[:, at]
        state_low, state_rest = halves(state)
        falling = dot_nn(fall, spread)
        across = falling * (
            dot_nn(b_map, state_low) + (dot_nn(b_low, state_low) + dot_nn(b_map, state_rest))
        )
        dv = dv_ref[:, at] + across
        u = u_ref[:, at]
        open_ = sigmoid(u)
        x = u * open_
        delta = dot_nn(steps, spread)
        v = x * delta
        v_low = v
        dy = dy_ref[:, at].astype(F32)
        dx = delta * dv + skip_ref[:, at] * dy
        ext_ref[0:LEN, at] = dx * (open_ * (1.0 + u * (1.0 - open_)))
        high_ref[:, at], low_ref[:, at] = halves(v_low * dv)
        x_ref[:, at] = (x * dv).astype(BF16)
        carried = local_ref[0, :, at] + pref_ref[0, :, at] * enter_ref[:, at].astype(F32)
        decay = dec_ref[0, :, at]
        end = jnp.sum(v_low * across, axis=0, keepdims=True) + decay * jnp.sum(
            state * carried, axis=0, keepdims=True
        )
        ends_ref[:, at] = jnp.broadcast_to(end, (8, WIDE))
        fall_v_ref[:, at], fall_rest_ref[:, at] = halves(falling * v)
        state_low_ref[:, at] = state_low
        rest_ref[:, at] = state_rest
        z, z_low = halves(dot_nn(grow, spread) * dy)
        state_ref[:, at] = keep * (decay * state + (dot_tn(c_map, z) + (dot_tn(c_low, z) + dot_tn(c_map, z_low))))
        return carry

    lax.fori_loop(0, width // WIDE, step, 0, unroll=3)
    select = select_ref[...]
    fall_v = fall_v_ref[...]
    state_low = state_low_ref[...]
    db_ref[...] = dot_nt(fall_v, state_low) + (
        dot_nt(fall_v, rest_ref[...]) + dot_nt(fall_rest_ref[...], state_low)
    )
    q_ref[...] = dot_nn(high_ref[...], select) + dot_nn(low_ref[...], select)
    r_ref[...] = dot_nn(x_ref[...], select)
    end_ref[0] = head_sums(ends_ref[...], select)

    def conv(i, carry):
        at = chunk(i, WIDE)
        ip = ip_ref[:, at]
        du = ext_ref[0:LEN, at]
        bias_grad_ref[:, at] += jnp.sum(du, axis=0, keepdims=True)
        total = taps_ref[3:4, at] * du
        taps_grad_ref[3:4, at] += jnp.sum(ip * du, axis=0, keepdims=True)
        for lag in range(1, 4):
            later = ext_ref[lag : lag + LEN, at]
            total = total + taps_ref[3 - lag : 4 - lag, at] * later
            taps_grad_ref[3 - lag : 4 - lag, at] += jnp.sum(ip * later, axis=0, keepdims=True)
        ig_ref[:, at] = total.astype(BF16)
        return carry

    lax.fori_loop(0, width // WIDE, conv, 0, unroll=4)

    @pl.when(c == 0)
    def _():
        head_ref[...] = ext_ref[0:8, :] * keep
        for lag in range(1, 4):
            part = keep * ext_ref[0:lag, :] * halo_ref[HALO - lag : HALO, :]
            taps_grad_ref[3 - lag : 4 - lag, :] += jnp.sum(part, axis=0, keepdims=True)


def place_kernel(moves, count, outs, where_ref, *refs):
    pieces, out_refs = refs[:count], refs[count : count + outs]
    stages, casts, sems = refs[count + outs : 2 * count + outs], refs[2 * count + outs : -1], refs[-1]
    loads = []
    for i, piece in enumerate(pieces):
        load = pltpu.make_async_copy(piece, stages[i], sems.at[0, i])
        load.start()
        loads.append(load)
    stores, waited = [], set()
    for n, (i, t, window, out, row_slot, col_slot) in enumerate(moves):
        if i not in waited:
            loads[i].wait()
            waited.add(i)
        first, rows, left, width = window
        source = stages[i].at[t, pl.ds(first, rows), pl.ds(left, width)]
        if casts:
            cast = casts[n]
            cast[...] = source[...].astype(cast.dtype)
            source = cast
        row = pl.multiple_of(where_ref[row_slot], 16)
        if width == out_refs[out].shape[1]:
            target = out_refs[out].at[pl.ds(row, rows)]
        else:
            col = pl.multiple_of(where_ref[col_slot], 128)
            target = out_refs[out].at[pl.ds(row, rows), pl.ds(col, width)]
        store = pltpu.make_async_copy(source, target, sems.at[1, n])
        store.start()
        stores.append(store)
    for store in stores:
        store.wait()


def place(pieces, moves, shapes, dtype):
    slots, fixed = [], []
    for i, t, window, which, row, col in moves:
        window = window or (0, pieces[i].shape[1], 0, pieces[i].shape[2])
        fixed.append((i, t, window, which, len(slots), len(slots) + 1))
        slots += [jnp.asarray(row, jnp.int32), jnp.asarray(col, jnp.int32)]
    anywhere = pl.BlockSpec(memory_space=pl.ANY)
    casts = []
    if dtype != pieces[0].dtype:
        casts = [pltpu.VMEM((w[1], w[3]), dtype) for _, _, w, _, _, _ in fixed]
    nbytes = sum(2 * 2 * a * b for a, b in shapes)
    return pl.pallas_call(
        functools.partial(place_kernel, fixed, len(pieces), len(shapes)),
        in_specs=[pl.BlockSpec(memory_space=pltpu.SMEM)] + [anywhere] * len(pieces),
        out_specs=[anywhere] * len(shapes),
        out_shape=[jax.ShapeDtypeStruct(shape, dtype) for shape in shapes],
        scratch_shapes=[pltpu.VMEM(piece.shape, piece.dtype) for piece in pieces]
        + casts
        + [pltpu.SemaphoreType.DMA((2, max(len(pieces), len(moves))))],
        compiler_params=pltpu.CompilerParams(vmem_limit_bytes=VMEM),
        cost_estimate=pl.CostEstimate(flops=0, bytes_accessed=nbytes, transcendentals=0),
        name="place",
    )(jnp.stack(slots), *pieces)


def norm_kernel(pieces_ref, gain_ref, hid_ref, normed_ref):
    parts, rows, width = pieces_ref.shape
    squares = jnp.zeros((rows, 128), F32)
    for t in range(parts):
        v = pieces_ref[t].astype(F32)
        squares = squares + fold(v * v)
    mean = jnp.sum(squares, axis=1, keepdims=True) / (width * parts)
    factor = lax.rsqrt(mean + EPSILON)
    for t in range(parts):
        at = slice(t * width, (t + 1) * width)
        v = pieces_ref[t]
        hid_ref[:, at] = v
        normed_ref[:, at] = (v.astype(F32) * factor * gain_ref[:, at]).astype(BF16)


def join_kernel(pieces_ref, live_ref, out_ref):
    parts, _, width = pieces_ref.shape
    for t in range(parts):
        live = live_ref[...]
        out_ref[:, t * width : (t + 1) * width] = (pieces_ref[t].astype(F32) * live).astype(BF16)


def swap(v, mask, count):
    return lax.ppermute(v, "dp", [(i, i ^ mask) for i in range(count)])


def exchange(v):
    return lax.all_to_all(v, "tensor", 0, 0, tiled=True)


def rotate(v, by, count):
    return lax.ppermute(v, "tensor", [(i, (i + by) % count) for i in range(count)])


def in_order(pieces, column):
    return jnp.roll(jnp.stack([pieces[0]] + pieces[:0:-1]), column, axis=0)


def same_core(count):
    return [list(range(0, count, 2)), list(range(1, count, 2))]


def gather_chips(v, count):
    return [(v, 0)] + [(swap(v, mask, count), mask) for mask in range(2, count, 2)]


def gather_core(mine, count):
    return mine + [(swap(a, 1, count), mask ^ 1) for a, mask in mine]


def gather_pieces(v, count):
    return gather_core(gather_chips(v, count), count)


ANYWHERE = pl.BlockSpec(memory_space=pl.ANY)


def unread(count, extra):
    return lambda kernel: lambda *refs: kernel(*refs[:count], *refs[count + extra :])


def after(v, *first):
    first = jax.tree.leaves(first)
    return pl.pallas_call(
        lambda *refs: None,
        in_specs=[ANYWHERE] * (1 + len(first)),
        out_specs=ANYWHERE,
        out_shape=jax.ShapeDtypeStruct(v.shape, v.dtype),
        input_output_aliases={0: 0},
        cost_estimate=pl.CostEstimate(flops=0, bytes_accessed=0, transcendentals=0),
        name="after",
    )(v, *first)


def pair_lanes(v):
    wide = jnp.pad(v, ((0, 0), (0, 64 - v.shape[1])))
    return jnp.concatenate([wide, wide], axis=1)


def local(
    dp_count, tensor_count,
    hidden_in, out_grad, seq_lengths, seq_device, seq_offset, norm_gain, w_gate, w_input, w_shared,
    w_step, conv_inner, conv_shared, conv_inner_bias, conv_shared_bias, step_bias, decay_log,
    skip_gain, gate_norm_gain, w_output,
):
    parts = tensor_count
    dp = lax.axis_index("dp")
    column = lax.axis_index("tensor")
    core, q = dp & 1, dp >> 1
    rows_dev, piece = hidden_in.shape
    rows = rows_dev // parts
    blocks = rows // LEN
    model = norm_gain.shape[0]
    shard = w_input.shape[1]
    inner = shard * parts
    heads_shard = w_step.shape[1]
    heads = heads_shard * parts
    width = inner // heads
    nstate = w_shared.shape[1] // 2
    groups = dp_count // 2

    aligned = piece % 128 == 0
    turn = jnp.stack([(column - d) % parts for d in range(parts)]).astype(jnp.int32)

    def send_rows(v, halo):
        pieces = []
        for t in range(parts):
            pieces.append(v[t * rows : (t + 1) * rows])
            if halo:
                start = max(t * rows, HALO)
                pieces.append(v[start - HALO : start])
        size = rows + (HALO if halo else 0)
        return exchange(jnp.concatenate(pieces, axis=0).reshape(parts, size, piece))

    def send_back(v):
        pieces = [v[:, t * piece : (t + 1) * piece] for t in range(parts)]
        return jnp.stack(pieces)

    def row_block(size):
        return max(n for n in range(16, 129, 16) if size % n == 0)

    def join(kernel, pieces, extra, extra_rows, outs):
        size = pieces.shape[1]
        block = row_block(size)
        extra_spec = (
            pl.BlockSpec((block, 1), lambda g: (g, 0))
            if extra_rows
            else pl.BlockSpec(extra.shape, lambda g: (0, 0))
        )
        wide = pl.BlockSpec((block, model), lambda g: (g, 0))
        return pl.pallas_call(
            kernel,
            grid=(size // block,),
            in_specs=[pl.BlockSpec((parts, block, piece), lambda g: (0, g, 0)), extra_spec],
            out_specs=[wide] * outs,
            out_shape=[jax.ShapeDtypeStruct((size, model), BF16)] * outs,
            compiler_params=pltpu.CompilerParams(vmem_limit_bytes=VMEM),
            cost_estimate=pl.CostEstimate(
                flops=0, bytes_accessed=size * model * 2 * (1 + outs), transcendentals=0
            ),
            name="join",
        )(pieces, extra)

    def join_plain(pieces):
        return jnp.concatenate([pieces[t] for t in range(parts)], axis=1)

    k_rows = model // dp_count
    out_rows = shard // dp_count

    def slices_of(index):
        return index & 1, index >> 1

    def gather_all(v):
        return lax.all_gather(v, ("dp", "tensor"), axis=0)

    def my_rows(w, size):
        return lax.dynamic_slice_in_dim(w, dp * size, size, 0)

    def place_columns(slices):
        moves = [
            (0, j, None, 0, j // parts * k_rows, j % parts * shard) for j in range(slices.shape[0])
        ]
        return place([slices], moves, [(model, inner)], BF16)[0]

    def place_output(slices):
        moves = [
            (0, j, None, 0, j % parts * shard + j // parts * out_rows, 0)
            for j in range(slices.shape[0])
        ]
        return place([slices], moves, [(inner, model)], BF16)[0]

    place_dp = core * (model // 2) + q * k_rows

    vectors = jnp.concatenate([step_bias, decay_log, skip_gain])
    vectors = jnp.pad(vectors, (0, shard - vectors.shape[0]))[None, :]
    small = jnp.concatenate(
        [conv_inner, conv_inner_bias[None, :], gate_norm_gain[None, :], vectors], axis=0
    )
    terms = []
    for _ in range(3):
        term = lax.reduce_precision(small, 8, 7)
        terms.append(term.astype(BF16))
        small = small - term
    step_rows = model * heads_shard // shard
    small = jnp.concatenate(terms + [w_step.reshape(step_rows, shard)], axis=0)
    small_rows = -(-small.shape[0] // 16) * 16
    small = jnp.pad(small, ((0, small_rows - small.shape[0]), (0, 0)))
    first = lax.dynamic_slice_in_dim(w_input, place_dp, k_rows, 0)
    first = jnp.concatenate([first, small], axis=0)
    first = [first] + [rotate(first, d, parts) for d in range(1, parts)]
    hid_pieces = send_rows(hidden_in, True)
    small = in_order([v[k_rows:] for v in first], column)
    in_pieces = gather_pieces(jnp.stack([v[:k_rows] for v in first]), dp_count)
    terms = small[:, :21].astype(F32).reshape(parts, 3, 7, shard)
    terms = (terms[:, 0] + terms[:, 1]) + terms[:, 2]
    by_shard = lambda v: jnp.swapaxes(v, 0, 1).reshape(v.shape[1], inner)
    taps = by_shard(terms[:, :4])
    inner_bias = by_shard(terms[:, 4:5])
    gain_out = by_shard(terms[:, 5:6])
    by_head = lambda i: terms[:, 6, i * heads_shard : (i + 1) * heads_shard].reshape(1, heads)
    steps_bias = pair_lanes(by_head(0))
    logs = pair_lanes(by_head(1))
    skip_wide = jnp.repeat(by_head(2), width, axis=1)
    w_steps = small[:, 21 : 21 + step_rows].reshape(parts, model, heads_shard)
    w_steps = jnp.swapaxes(w_steps, 0, 1).reshape(model, heads)
    w_misc = jnp.concatenate([w_shared, pair_lanes(w_steps)], axis=1)
    misc_width = w_misc.shape[1]

    block_start = column * rows + jnp.arange(blocks + 1, dtype=jnp.int32) * LEN
    inside = (
        (seq_device[None, :] == dp)
        & (block_start[:, None] >= seq_offset[None, :])
        & (block_start[:, None] < seq_offset[None, :] + seq_lengths[None, :])
    )
    offset = jnp.sum(jnp.where(inside, block_start[:, None] - seq_offset[None, :], 0), axis=1)
    keep = (offset > 0).astype(jnp.int32)
    live_blocks = jnp.sum(inside.astype(F32), axis=1)[:blocks]
    live = jnp.repeat(live_blocks, LEN)[:, None]
    dev_start = jnp.arange(rows_dev // LEN, dtype=jnp.int32) * LEN
    dev_inside = (
        (seq_device[None, :] == dp)
        & (dev_start[:, None] >= seq_offset[None, :])
        & (dev_start[:, None] < seq_offset[None, :] + seq_lengths[None, :])
    )
    live_dev = jnp.repeat(jnp.sum(dev_inside.astype(F32), axis=1), LEN)[:, None]

    lane_head = jnp.arange(inner, dtype=jnp.int32) // width
    half_index = jnp.arange(128, dtype=jnp.int32) % 64
    spread = (half_index[:, None] == lane_head[None, :]).astype(BF16)
    select = (lane_head[:, None] == jnp.arange(128, dtype=jnp.int32)[None, :]).astype(BF16)
    columns = (
        (jnp.arange(192, dtype=jnp.int32) % 64)[:, None]
        == (jnp.arange(heads * LEN, dtype=jnp.int32) // LEN)[None, :]
    ).astype(BF16)

    if aligned:
        hid, normed_all = join(norm_kernel, hid_pieces, norm_gain[None, :], False, 2)
    else:
        hid = join_plain(hid_pieces)
        wide_in = hid.astype(F32)
        mean = jnp.mean(wide_in * wide_in, axis=1, keepdims=True)
        normed_all = (wide_in * lax.rsqrt(mean + EPSILON) * norm_gain[None, :]).astype(BF16)
    normed = normed_all[:rows]
    misc = dot_nn(normed_all, w_misc)

    params = pltpu.CompilerParams(vmem_limit_bytes=VMEM)
    smem = pl.BlockSpec(memory_space=pltpu.SMEM)
    full = lambda *shape: pl.BlockSpec(shape, lambda g: (0,) * len(shape))
    up = lambda *shape: pl.BlockSpec(shape, lambda g: (g,) + (0,) * (len(shape) - 1))
    down = lambda *shape: pl.BlockSpec(
        shape, lambda g: (blocks - 1 - g,) + (0,) * (len(shape) - 1)
    )
    out = jax.ShapeDtypeStruct
    cost = lambda flops, size: pl.CostEstimate(
        flops=flops, bytes_accessed=size, transcendentals=rows * inner
    )
    halo_block = lambda cols: pl.BlockSpec((HALO, cols), lambda g: (rows // HALO, 0))
    wide_map = 2 * rows * inner * nstate
    lanes = out((rows, 128), F32)

    (
        shared_u, b_map, c_map, delta2, slope2, rate2, cum3, cum_t, grow2, fall2, coef2, dec2,
    ) = pl.pallas_call(
        maps_kernel,
        grid=(blocks,),
        in_specs=[
            smem, up(LEN, misc_width), halo_block(misc_width), full(4, 2 * nstate),
            full(1, 2 * nstate), full(1, 128), full(1, 128),
        ],
        out_specs=[up(LEN, 2 * nstate)]
        + [up(LEN, 128)] * 5
        + [up(LEN, 192), pl.BlockSpec((128, LEN), lambda g: (0, g))]
        + [up(LEN, 128)] * 3
        + [up(1, 1, 128)],
        out_shape=[out((rows, 2 * nstate), F32)]
        + [lanes] * 5
        + [out((rows, 192), F32), out((128, rows), F32)]
        + [lanes] * 3
        + [out((blocks, 1, 128), F32)],
        scratch_shapes=[pltpu.VMEM((LEN + 8, 2 * nstate), F32)],
        compiler_params=params,
        cost_estimate=cost(0, rows * 128 * 4 * 16),
        name="maps",
    )(keep, misc, misc, conv_shared, conv_shared_bias[None, :], steps_bias, logs)

    moves = []
    for i, (_, mask) in enumerate(in_pieces):
        c2, q2 = slices_of(dp ^ mask)
        row = c2 * (model // 2) + q2 * k_rows
        moves += [(i, d, None, 0, row, turn[d] * shard) for d in range(parts)]
    moves.append((len(in_pieces), 0, None, 0, 0, inner))
    (w_in,) = place(
        [a for a, _ in in_pieces] + [w_misc[None]], moves, [(model, inner + misc_width)], BF16
    )
    gate_slices = gather_all(after(my_rows(w_gate, k_rows), *first[1:]))
    out_slices = None
    if out_rows % 16 == 0:
        out_slices = gather_all(after(my_rows(w_output, out_rows), *first[1:]))
    grad_pieces = send_rows(out_grad, False)
    inner_proj = dot_nn(normed_all, w_in[:, :inner])


    u, local_states, chunk_state, dec_wide, pref_wide, through = pl.pallas_call(
        conv_states_kernel,
        grid=(blocks,),
        in_specs=[
            smem, up(LEN, inner), halo_block(inner), full(4, inner), full(1, inner),
            up(LEN, nstate), up(LEN, 128), up(1, 1, 128), full(128, inner),
        ],
        out_specs=[
            up(LEN, inner), up(1, nstate, inner), full(nstate, inner), up(1, 1, inner),
            up(1, 1, inner), full(1, inner),
        ],
        out_shape=[
            out((rows, inner), F32), out((blocks, nstate, inner), F32), out((nstate, inner), F32),
            out((blocks, 1, inner), F32), out((blocks, 1, inner), F32), out((1, inner), F32),
        ],
        scratch_shapes=[
            pltpu.VMEM((LEN + 8, inner), F32), pltpu.VMEM((nstate, inner), F32),
            pltpu.VMEM((1, inner), F32),
        ],
        compiler_params=params,
        cost_estimate=cost(2 * wide_map, rows * inner * 12),
        name="conv_states",
    )(keep, inner_proj, inner_proj, taps, inner_bias, b_map, coef2, dec2, spread)

    to_right = [(i, i + 1) for i in range(parts - 1)]
    to_left = [(i + 1, i) for i in range(parts - 1)]
    entering = lax.ppermute(chunk_state.astype(BF16), "tensor", to_right)

    heads_t = pl.BlockSpec((128, LEN), lambda g: (0, g))
    y_within = pl.pallas_call(
        within_kernel,
        grid=(blocks,),
        in_specs=[
            up(LEN, inner), up(LEN, 192), heads_t, up(LEN, 128), up(LEN, nstate),
            up(LEN, nstate), full(192, heads * LEN), full(128, inner),
        ],
        out_specs=up(LEN, inner),
        out_shape=out((rows, inner), F32),
        compiler_params=params,
        cost_estimate=cost(8 * wide_map, rows * inner * 8),
        name="within",
    )(
        u, cum3, cum_t, delta2, b_map, c_map, columns, spread
    )

    w_gates = place_columns(gate_slices)
    gate_proj = dot_nn(normed, w_gates)
    beside = [y_within, gate_proj]
    for i in range(parts - 2):
        entering = after(entering, *beside[i : i + 1])
        entering = lax.ppermute(
            (chunk_state + through * entering.astype(F32)).astype(BF16), "tensor", to_right
        )
    if out_slices is None:
        w_out = lax.all_gather(w_output, "tensor", axis=0, tiled=True)
    else:
        w_out = place_output(out_slices)

    if aligned:
        (masked,) = join(join_kernel, grad_pieces, live, True, 1)
    else:
        masked = join_plain(grad_pieces) * live.astype(BF16)
    normed_y_grad = dot_nt(masked, w_out)

    normed_y, scan_grad, gate_grad, q_plus, dc_across, gain_out_grad, skip_lanes, chunk_grad = (
        pl.pallas_call(
            gate_kernel,
            grid=(blocks,),
            in_specs=[
                smem, down(LEN, inner), down(LEN, inner), down(LEN, inner), down(LEN, inner),
                down(1, nstate, inner), full(nstate, inner), down(1, 1, inner), down(LEN, nstate),
                down(LEN, 128), full(1, inner), full(1, inner), down(1, 1, inner),
                full(128, inner), full(inner, 128),
            ],
            out_specs=[
                down(LEN, inner), down(LEN, inner), down(LEN, inner), down(LEN, 128),
                down(LEN, nstate), full(1, inner), full(1, inner), full(nstate, inner),
            ],
            out_shape=[
                out((rows, inner), BF16), out((rows, inner), F32), out((rows, inner), BF16),
                lanes, out((rows, nstate), F32), out((1, inner), F32),
                out((1, inner), F32), out((nstate, inner), F32),
            ],
            scratch_shapes=[
                pltpu.VMEM((LEN, inner), F32), pltpu.VMEM((nstate, inner), BF16),
                pltpu.VMEM((nstate, inner), F32),
            ]
            + [pltpu.VMEM((LEN, inner), BF16)] * 5,
            compiler_params=params,
            cost_estimate=cost(6 * wide_map, rows * inner * 24),
            name="gate",
        )(
            keep, y_within, u, gate_proj, normed_y_grad, local_states, entering, pref_wide, c_map,
            grow2, skip_wide, gain_out, dec_wide, spread, select,
        )
    )

    leaving = lax.ppermute(chunk_grad.astype(BF16), "tensor", to_left)

    def half_of(v, which):
        size = v.shape[1] // 2
        return lax.dynamic_slice_in_dim(v, which * size, size, 1)

    out_sent = swap(dot_tn(normed_y, half_of(masked, 1 - core)).astype(BF16), 1, dp_count)
    gate_sent = swap(dot_tn(half_of(normed, 1 - core), gate_grad).astype(BF16), 1, dp_count)
    gate_part = dot_nt(gate_grad, w_gates)
    mixed_rows = dot_nn(normed_y, w_out).astype(BF16)
    out_total = (dot_tn(normed_y, half_of(masked, core)) + out_sent.astype(F32)).astype(BF16)
    beside = [[gate_part], [out_total, mixed_rows]]
    for i in range(parts - 2):
        leaving = after(leaving, *(beside[i] if i < len(beside) else []))
        if i == 1:
            mixed_sent = after(send_back(mixed_rows), leaving)
        leaving = lax.ppermute(
            (chunk_grad + through * leaving.astype(F32)).astype(BF16), "tensor", to_left
        )
    gate_total = (dot_tn(half_of(normed, core), gate_grad) + gate_sent.astype(F32)).astype(BF16)
    out_group = shard // groups
    group_rows = model // dp_count
    half_model = model // 2

    def chip_sum(v):
        return lax.psum_scatter(
            v, "dp", scatter_dimension=0, axis_index_groups=same_core(dp_count), tiled=False
        )

    def shard_sum(v):
        mine = lax.psum_scatter(v, "tensor", scatter_dimension=0, tiled=False)
        return lax.all_gather(mine, "dp", axis=0)

    out_sum = chip_sum(
        jnp.swapaxes(out_total.reshape(parts, groups, out_group, half_model), 0, 1)
    )
    gate_sum = chip_sum(gate_total.reshape(groups, group_rows, inner))
    out_parts = shard_sum(out_sum)
    gate_parts = shard_sum(
        jnp.stack([gate_sum[:, t * shard : (t + 1) * shard] for t in range(parts)])
    )

    dv_within, db_within, dc_within = pl.pallas_call(
        unread(9, 1)(within_back_kernel),
        grid=(blocks,),
        in_specs=[
            up(LEN, inner), up(LEN, inner), up(LEN, 192), heads_t, up(LEN, 128), up(LEN, nstate),
            up(LEN, nstate), full(192, heads * LEN), full(128, inner), ANYWHERE,
        ],
        out_specs=[up(LEN, inner), up(LEN, nstate), up(LEN, nstate)],
        out_shape=[out((rows, inner), F32), out((rows, nstate), F32), out((rows, nstate), F32)],
        compiler_params=params,
        cost_estimate=cost(16 * wide_map, rows * inner * 10),
        name="within_back",
    )(u, scan_grad, cum3, cum_t, delta2, b_map, c_map, columns, spread, gate_part)


    grads, db_across, q_minus, step_sums, end_sums, taps_grad, bias_grad, head_rows = (
        pl.pallas_call(
            across_back_kernel,
            grid=(blocks,),
            in_specs=[
                smem, down(LEN, inner), down(LEN, inner), down(LEN, inner), down(LEN, inner),
                halo_block(inner), down(1, nstate, inner), full(nstate, inner), down(1, 1, inner),
                full(nstate, inner), down(LEN, nstate), down(LEN, nstate), down(LEN, 128),
                down(LEN, 128), down(LEN, 128), full(1, inner), down(1, 1, inner), full(4, inner),
                full(128, inner), full(inner, 128),
            ],
            out_specs=[
                down(LEN, inner), down(LEN, nstate), down(LEN, 128), down(LEN, 128),
                down(1, 8, 128), full(4, inner), full(1, inner), full(8, inner),
            ],
            out_shape=[
                out((rows, inner + misc_width), BF16), out((rows, nstate), F32), lanes, lanes,
                out((blocks, 8, 128), F32), out((4, inner), F32), out((1, inner), F32),
                out((8, inner), F32),
            ],
            scratch_shapes=[
                pltpu.VMEM((nstate, inner), F32), pltpu.VMEM((LEN + 8, inner), F32),
            ]
            + [pltpu.VMEM((LEN, inner), BF16)] * 7
            + [pltpu.VMEM((8, inner), F32)],
            compiler_params=params,
            cost_estimate=cost(6 * wide_map, rows * inner * 20),
            name="across_back",
        )(
            keep, u, scan_grad, dv_within, inner_proj, inner_proj, local_states,
            entering, pref_wide, after(leaving, dv_within, gate_total), b_map, c_map, grow2, fall2, delta2, skip_wide, dec_wide, taps,
            spread, select,
        )
    )

    misc_at = inner // misc_width
    mixer_part = exchange(mixed_sent)
    grads, shared_taps_grad, shared_bias_grad, shared_head, vectors = pl.pallas_call(
        unread(17, 1)(maps_back_kernel),
        grid=(blocks,),
        in_specs=[
            smem, down(LEN, nstate), down(LEN, nstate), down(LEN, nstate), down(LEN, nstate),
            down(LEN, 2 * nstate), down(LEN, misc_width), halo_block(misc_width),
            full(4, 2 * nstate), down(LEN, 128), down(LEN, 128), down(LEN, 128), down(1, 8, 128),
            down(LEN, 128), down(LEN, 128), full(1, 128), ANYWHERE, ANYWHERE,
        ],
        out_specs=[
            pl.BlockSpec((LEN, misc_width), lambda g: (blocks - 1 - g, misc_at)),
            full(4, 2 * nstate), full(1, 2 * nstate), full(8, 2 * nstate), full(8, 128),
        ],
        out_shape=[
            out((rows, inner + misc_width), BF16), out((4, 2 * nstate), F32),
            out((1, 2 * nstate), F32), out((8, 2 * nstate), F32), out((8, 128), F32),
        ],
        input_output_aliases={16: 0},
        scratch_shapes=[pltpu.VMEM((LEN + 8, 2 * nstate), F32)],
        compiler_params=params,
        cost_estimate=cost(0, rows * 128 * 4 * 16),
        name="maps_back",
    )(
        keep, db_within, db_across, dc_within, dc_across, shared_u, misc, misc, conv_shared,
        q_plus, q_minus, step_sums, end_sums, slope2, rate2, logs, grads, mixer_part,
    )
    mixer_part = mixer_part.reshape(rows_dev, piece).astype(F32)
    mixed_out = (hidden_in.astype(F32) + live_dev * mixer_part).astype(BF16)

    next_heads = lax.ppermute(
        jnp.concatenate([head_rows, shared_head], axis=1), "tensor", to_left
    )
    all_taps = jnp.concatenate([taps, conv_shared], axis=1)
    reach = inner + 2 * nstate
    last_rows = lax.dynamic_slice(grads, (rows - 16, 0), (16, reach)).astype(F32)
    for lag in range(1, 4):
        moved = jnp.pad(next_heads[:lag], ((16 - lag, 0), (0, 0)))
        last_rows = last_rows + all_taps[3 - lag][None, :] * moved
    grads = lax.dynamic_update_slice(grads, last_rows.astype(BF16), (rows - 16, 0))

    in_sent = swap(dot_tn(half_of(normed, 1 - core), grads).astype(BF16), 1, dp_count)
    normed_grad = gate_part + dot_nt(grads, w_in)
    input_grad, norm_gain_grad = pl.pallas_call(
        input_grad_kernel,
        grid=(blocks,),
        in_specs=[up(LEN, model), up(LEN, model), full(1, model)],
        out_specs=[up(LEN, model), full(1, model)],
        out_shape=[out((rows, model), BF16), out((1, model), F32)],
        compiler_params=params,
        cost_estimate=cost(0, rows * model * 8),
        name="input_grad",
    )(normed_grad, hid, norm_gain[None, :])

    tiny = jnp.concatenate(
        [
            shared_taps_grad.reshape(1, -1), shared_bias_grad, vectors[0:1], vectors[1:2],
            norm_gain_grad,
        ],
        axis=1,
    )
    tiny = jnp.pad(tiny, ((0, 0), (0, inner - tiny.shape[1])))
    tiny = jnp.concatenate([taps_grad, bias_grad, gain_out_grad, skip_lanes, tiny], axis=0)
    tiny = tiny + swap(tiny, 1, dp_count)

    def two_terms(v):
        high = lax.reduce_precision(v, 8, 7)
        return jnp.concatenate([high, v - high], axis=0).astype(BF16)

    def one_term(v):
        return v[:8].astype(F32) + v[8:].astype(F32)

    in_total = (dot_tn(half_of(normed, core), grads) + in_sent.astype(F32)).astype(BF16)
    tiny_low = jnp.pad(two_terms(tiny), ((0, 0), (0, misc_width)))
    in_part = lambda which: jnp.concatenate(
        [lax.dynamic_slice_in_dim(in_total, which * k_rows, k_rows, 0), tiny_low], axis=0
    )
    in_received = [in_part(q)]
    for mask in range(1, groups):
        in_received.append(swap(in_part(q ^ mask), 2 * mask, dp_count))
    tiny = [one_term(v[k_rows:, :inner]) for v in in_received]
    while len(tiny) > 1:
        tiny = [tiny[i] + tiny[i + 1] for i in range(0, len(tiny), 2)]
    tiny_low = two_terms(tiny[0])
    in_group = in_received[0][:k_rows].astype(F32)
    for v in in_received[1:]:
        in_group = in_group + v[:k_rows].astype(F32)
    in_group = in_group.astype(BF16)
    cols = shard + misc_width
    lengths = -(-inner // cols)
    tiny_low = jnp.pad(tiny_low, ((0, 0), (0, lengths * cols - inner)))
    tiny_low = jnp.concatenate([tiny_low[:, i * cols : (i + 1) * cols] for i in range(lengths)])
    in_sends = []
    for t in range(parts):
        mine = [in_group[:, t * shard : (t + 1) * shard], in_group[:, inner:]]
        in_sends.append(jnp.concatenate([jnp.concatenate(mine, axis=1), tiny_low], axis=0))
    hidden_sent = send_back(input_grad)
    hidden_part = exchange(hidden_sent)
    in_arrived = exchange(jnp.stack(in_sends))
    in_shard = jnp.sum(in_arrived[:, :k_rows].astype(F32), axis=0).astype(BF16)
    tiny_low = in_arrived[:, k_rows:].reshape(parts, lengths, 2, 8, cols).astype(F32)
    tiny = jnp.sum(tiny_low[:, :, 0] + tiny_low[:, :, 1], axis=0)
    tiny = jnp.concatenate([tiny[i] for i in range(lengths)], axis=1)
    own_columns = lax.dynamic_slice_in_dim(tiny[:7], column * shard, shard, 1)
    ends_at = [0]
    for size in (8 * nstate, 2 * nstate, 128, 128, model):
        ends_at.append(ends_at[-1] + size)
    part = lambda i: tiny[7, ends_at[i] : ends_at[i + 1]]
    own_heads = lambda v: lax.dynamic_slice_in_dim(v, column * heads_shard, heads_shard, 0)

    w_output_grad = (
        out_parts.reshape(groups, 2, out_group, half_model)
        .transpose(0, 2, 1, 3)
        .reshape(shard, model)
        .astype(F32)
    )
    w_gate_grad = (
        gate_parts.reshape(groups, 2, group_rows, shard)
        .transpose(1, 0, 2, 3)
        .reshape(model, shard)
        .astype(F32)
    )
    in_pieces = gather_pieces(in_shard[None], dp_count)
    moves = []
    for i, (_, mask) in enumerate(in_pieces):
        c2, q2 = slices_of(dp ^ mask)
        row = c2 * half_model + q2 * k_rows
        moves.append((i, 0, (0, k_rows, 0, shard), 0, row, 0))
        moves.append((i, 0, (0, k_rows, shard, 2 * nstate), 1, row, 0))
        moves.append((i, 0, (0, k_rows, shard + 2 * nstate, 128), 2, row, 0))
    w_input_grad, w_shared_grad, step_lanes = place(
        [a for a, _ in in_pieces],
        moves,
        [(model, shard), (model, 2 * nstate), (model, 128)],
        F32,
    )
    w_step_grad = lax.dynamic_slice_in_dim(step_lanes, column * heads_shard, heads_shard, 1)
    hidden_grad = hidden_part.reshape(rows_dev, piece).astype(F32) + out_grad.astype(F32)

    return (
        mixed_out,
        hidden_grad,
        part(4),
        w_gate_grad,
        w_input_grad,
        w_shared_grad,
        w_step_grad,
        own_columns[:4],
        part(0).reshape(4, 2 * nstate),
        own_columns[4],
        part(1),
        own_heads(part(2)),
        own_heads(part(3)),
        jnp.sum(own_columns[6].reshape(heads_shard, width), axis=1),
        own_columns[5],
        w_output_grad,
    )


def solution(mesh):
    split = P("tensor")
    in_specs = (
        P("dp", "tensor"), P("dp", "tensor"), P(), P(), P(), P(), P(None, "tensor"),
        P(None, "tensor"), P(), P(None, "tensor"), P(None, "tensor"), P(), split, P(), split,
        split, split, split, P("tensor", None),
    )
    out_specs = (
        P("dp", "tensor"), P("dp", "tensor"), P(), P(None, "tensor"), P(None, "tensor"), P(),
        P(None, "tensor"), P(None, "tensor"), P(), split, P(), split, split, split, split,
        P("tensor", None),
    )
    body = functools.partial(local, mesh.shape["dp"], mesh.shape["tensor"])
    return jax.shard_map(body, mesh=mesh, in_specs=in_specs, out_specs=out_specs, check_vma=False)
```
